32 devices in a mesh: gx: 16 (over z, y, x), gy: 2 (over core).
Axes of the slice: x: 2, y: 2, z: 4, core: 2. Of those that a mesh axis runs over, the one named last changes fastest.
Arguments:
- skip_feature_rows: bfloat16 [64, 192, 512], P(('gx', 'gy')), may hold values from -6 to 6
- coarse_features: bfloat16 [64, 192, 512], P(('gx', 'gy')), may hold values from -6 to 6
- cotangent: bfloat16 [64, 192, 512], P(('gx', 'gy')), may hold values from -6 to 6
- fine_coords: int32 [64, 3], P(('gx', 'gy')), may hold values from 0 to 3, as said below
- coarse_coords: int32 [64, 3], P(('gx', 'gy')), may hold values from 0 to 1, as said below
- parents: int32 [64], P(('gx', 'gy')), may hold values from 0 to 1
- counts: int32 [32], P(('gx', 'gy')), may hold values from 1 to 2
- conv_weight: bfloat16 [192, 27, 192], replicated, may hold values from -0.078125 to 0.078125
- up_weight: bfloat16 [8, 192, 192], replicated, may hold values from -0.4375 to 0.4375
Outputs:
- grad_skip: bfloat16 [64, 192, 512], P(('gx', 'gy'))
- grad_coarse: bfloat16 [64, 192, 512], P(('gx', 'gy'))
- grad_conv: float32 [192, 27, 192], P('gy')
The draws below stay inside these ranges and needn't reach their ends.
Inputs may be any that keep to these rules, and one draw needn't show every extreme that they name: `fine_coords`: within one tile the fine slots have distinct coordinates in 0..1, 0..1, 0..3, and each equals 2 coarse_coords of its parent plus a 0/1 offset per axis. `coarse_coords`: within one tile the 2 coarse slots hold each coarse block position of the tile once.
All inputs are finite; a program needn't handle non-finite values.
Results may differ from the reference program's by a relative error of at most 0.013.
Values may be sent and summed in bfloat16 or wider, within the bound.
A program may use at most 128 MiB of HBM per device.

```python
import jax
import jax.numpy as jnp
from jax import lax

CH = 192
NB = 2
FB_X = 2
FB_Y = 2
FB_Z = 4
NC = 2
SLOTS = 64
COARSE_SLOT_ALL = 64
N_GX = 16
N_GY = 2


def geometry(key):
    tile_count = N_GX * N_GY
    tile_keys = jax.random.split(jax.random.fold_in(key, 11), tile_count)
    coarse_y = FB_Y // 2
    coarse_z = FB_Z // 2

    def one_tile(tile_key):
        key_pos, key_par, key_oct = jax.random.split(tile_key, 3)
        position = jax.random.permutation(key_pos, NC).astype(jnp.int32)
        coarse = jnp.stack([position // (coarse_y * coarse_z), position // coarse_z % coarse_y, position % coarse_z], 1)
        parent_ids = jax.random.randint(key_par, (NB,), 0, NC, dtype=jnp.int32)
        octant_ids = jax.random.permutation(key_oct, 8).astype(jnp.int32)[:NB]
        octant = jnp.stack([octant_ids // 4, octant_ids // 2 % 2, octant_ids % 2], 1)
        fine = 2 * coarse[parent_ids] + octant
        return (coarse, fine, parent_ids)
    coarse, fine, parent_ids = jax.vmap(one_tile)(tile_keys)
    return (coarse.reshape(tile_count * NC, 3), fine.reshape(tile_count * NB, 3), parent_ids.reshape(tile_count * NB))


def draw_fine_coords(key, part):
    return geometry(key)[1]


def draw_coarse_coords(key, part):
    return geometry(key)[0]


def draw_parents(key, part):
    return geometry(key)[2]


def draw_counts(key, part):
    tile_count = N_GX * N_GY
    drawn = jax.random.randint(jax.random.fold_in(key, 23), (tile_count,), 1, NB + 1, dtype=jnp.int32)
    return drawn.at[0].set(NB)


def raised(values, own_key, source, target, shards_of, factor):
    owner, partner = [(jnp.arange(values.shape[dim]) // (values.shape[dim] // shards_of)).reshape([-1 if axis == dim else 1 for axis in range(values.ndim)]) for dim in (source, target)]
    chosen = jax.random.permutation(own_key, shards_of)[partner]
    strong = (owner == chosen) | (owner == (partner + shards_of // 2) % shards_of)
    return jnp.where(strong, factor * values, values)


def level_of(stream_key, shape, cuts, low, high):
    def one(dim, shards_of):
        draws = jax.random.uniform(jax.random.fold_in(jax.random.fold_in(stream_key, 6), dim), (shards_of,), jnp.float32, low / len(cuts), high / len(cuts))
        return jnp.repeat(jnp.exp(draws), shape[dim] // shards_of).reshape((-1,) + (1,) * (len(shape) - dim - 1))

    level = one(*cuts[0])
    for cut in cuts[1:]:
        level = level * one(*cut)
    return level


def normal_values(rng, shape, scale, bound, pieces=(), kind=jnp.bfloat16):
    loudness = level_of(rng, shape, pieces, -0.22, 0.18) if pieces else 1.0
    result = jax.random.normal(rng, shape, jnp.float32) * scale * loudness
    return jnp.minimum(jnp.maximum(result, -bound), bound).astype(kind)


def gaussian_with(own_key, extent, deviation, reach, pieces, heavy, held_as=jnp.bfloat16):
    values = deviation * jax.random.normal(own_key, extent, jnp.float32)
    if pieces:
        values = values * level_of(own_key, extent, pieces, -0.22, 0.18)
    return jnp.clip(raised(values, jax.random.fold_in(own_key, 3), *heavy), -reach, reach).astype(held_as)


def setup_inputs(seed: int = 0) -> dict:
    streams_of = jax.random.split(jax.random.key(seed), 10)
    return {
        "skip_feature_rows": normal_values(streams_of[0], (SLOTS, CH, 512), 1.0, 6.0, ((0, 32),)),
        "coarse_features": normal_values(streams_of[1], (COARSE_SLOT_ALL, CH, 512), 1.0, 6.0, ((0, 32),)),
        "cotangent": gaussian_with(streams_of[2], (SLOTS, CH, 512), 1.0, 6.0, ((0, 32),), (0, 1, 32, 2.75)),
        "fine_coords": draw_fine_coords(jax.random.fold_in(streams_of[9], 71), 0),
        "coarse_coords": draw_coarse_coords(jax.random.fold_in(streams_of[9], 71), 0),
        "parents": draw_parents(jax.random.fold_in(streams_of[9], 71), 0),
        "counts": draw_counts(jax.random.fold_in(streams_of[9], 71), 0),
        "conv_weight": normal_values(streams_of[7], (CH, 27, CH), (27 * CH) ** -0.5, 0.078125),
        "up_weight": normal_values(streams_of[8], (8, CH, CH), CH ** -0.5, 0.4375),
    }


def index_tuple(anchor):
    return tuple(jnp.asarray(entry).astype(jnp.int32) for entry in anchor)


def add_into(target, addend, anchor):
    anchor = index_tuple(anchor)
    current = lax.dynamic_slice(target, anchor, addend.shape)
    return lax.dynamic_update_slice(target, current + addend, anchor)


def upsample(coarse_row, octant, up_rows):
    channel_count = coarse_row.shape[0]
    block_cube = coarse_row.reshape(channel_count, 8, 8, 8)
    octant_cube = lax.dynamic_slice(block_cube, index_tuple((0, 4 * octant[0], 4 * octant[1], 4 * octant[2])), (channel_count, 4, 4, 4))
    product = jnp.dot(up_rows.astype(jnp.float32), octant_cube.reshape(channel_count, 64).astype(jnp.float32),
                      precision=lax.Precision.HIGHEST)
    product = product.reshape(2, 2, 2, channel_count, 4, 4, 4).transpose(3, 4, 0, 5, 1, 6, 2)
    return product.reshape(channel_count, 512)


def fold_down(grad_row, up_rows):
    channel_count = grad_row.shape[0]
    regrouped = grad_row.reshape(channel_count, 4, 2, 4, 2, 4, 2).transpose(2, 4, 6, 0, 1, 3, 5).reshape(8 * channel_count, 64)
    return lax.dot_general(up_rows.astype(jnp.float32), regrouped.astype(jnp.float32), (((0,), (0,)), ((), ())),
                           precision=lax.Precision.HIGHEST)


def coarse_gradient(grad_rows, parent_ids, octants, coarse_count, up_rows):
    channel_count = grad_rows.shape[1]
    coarse_total = jnp.zeros((coarse_count, channel_count, 8, 8, 8), jnp.float32)
    for member in range(grad_rows.shape[0]):
        addend = fold_down(grad_rows[member], up_rows).reshape(1, channel_count, 4, 4, 4)
        anchor = (parent_ids[member], 0, 4 * octants[member, 0], 4 * octants[member, 1], 4 * octants[member, 2])
        coarse_total = add_into(coarse_total, addend, anchor)
    return coarse_total.astype(jnp.bfloat16).reshape(coarse_count, channel_count, 512)


def columns(padded, coord, reverse):
    channel_count = padded.shape[0]
    window = lax.dynamic_slice(padded, index_tuple((0, 8 * coord[0], 8 * coord[1], 8 * coord[2])), (channel_count, 10, 10, 10))
    shifted = []
    for step_x in range(3):
        for step_y in range(3):
            for step_z in range(3):
                if reverse:
                    first_x, first_y, first_z = 2 - step_x, 2 - step_y, 2 - step_z
                else:
                    first_x, first_y, first_z = step_x, step_y, step_z
                view = window[:, first_x:first_x + 8, first_y:first_y + 8, first_z:first_z + 8]
                shifted.append(view.reshape(channel_count, 512))
    return jnp.concatenate(shifted, 0)


def forward_slot(hidden_cols, cot_row, occupied, weight_flat):
    pre = jnp.dot(weight_flat.astype(jnp.float32), hidden_cols.astype(jnp.float32), precision=lax.Precision.HIGHEST)
    sigma = jax.nn.sigmoid(pre)
    return (cot_row.astype(jnp.float32) * (sigma * (1.0 + pre * (1.0 - sigma))) * occupied).astype(jnp.bfloat16)


def tile_frame(grid_vals, grid_coords, tile_x, tile_y):
    channel_count = grid_vals.shape[3]
    wide = jnp.zeros((channel_count, 24 * FB_X, 24 * FB_Y, 8 * FB_Z + 2), jnp.bfloat16)
    for shift_x in (-1, 0, 1):
        for shift_y in (-1, 0, 1):
            near_x = tile_x + shift_x
            near_y = tile_y + shift_y
            inside = (near_x >= 0) & (near_x < N_GX) & (near_y >= 0) & (near_y < N_GY)
            clamp_x = jnp.clip(near_x, 0, N_GX - 1)
            clamp_y = jnp.clip(near_y, 0, N_GY - 1)
            features = grid_vals[clamp_x, clamp_y] * inside.astype(jnp.bfloat16)
            placed = grid_coords[clamp_x, clamp_y]
            for member in range(NB):
                anchor = (0, 8 * FB_X * (shift_x + 1) + 8 * placed[member, 0],
                          8 * FB_Y * (shift_y + 1) + 8 * placed[member, 1], 1 + 8 * placed[member, 2])
                wide = add_into(wide, features[member].reshape(channel_count, 8, 8, 8), anchor)
    return wide[:, 8 * FB_X - 1:16 * FB_X + 1, 8 * FB_Y - 1:16 * FB_Y + 1, :]


def reference(skip_feature_rows, coarse_features, cotangent, fine_coords, coarse_coords, parents, counts, conv_weight, up_weight):
    tile_count = N_GX * N_GY
    tile_ids = jnp.arange(tile_count, dtype=jnp.int32)
    slot_ids = jnp.arange(tile_count * NB, dtype=jnp.int32)
    owner_tile = slot_ids // NB
    occupied = (slot_ids % NB < counts[owner_tile]).astype(jnp.float32)
    up_rows = up_weight.reshape(8 * CH, CH)
    parent_rows = (owner_tile * NC + parents).astype(jnp.int32)
    octants = (fine_coords - 2 * coarse_coords[parent_rows]).astype(jnp.int32)
    lifted = jax.vmap(lambda coarse_row, octant: upsample(coarse_row, octant, up_rows))(coarse_features[parent_rows], octants)
    hidden = ((lifted + skip_feature_rows.astype(jnp.float32)) * occupied[:, None, None]).astype(jnp.bfloat16)
    hidden_grid = hidden.reshape(N_GX, N_GY, NB, CH, 512)
    coord_grid = fine_coords.reshape(N_GX, N_GY, NB, 3)
    cot_grid = cotangent.reshape(tile_count, NB, CH, 512)
    occupied_grid = occupied.reshape(tile_count, NB)
    weight_flat = conv_weight.reshape(CH, 27 * CH)
    weight_flipped = jnp.transpose(conv_weight, (2, 1, 0)).reshape(CH, 27 * CH)

    def first_pass(weight_sum, tile):
        tile_x = tile // N_GY
        tile_y = tile % N_GY
        padded = tile_frame(hidden_grid, coord_grid, tile_x, tile_y)
        own_coords = coord_grid[tile_x, tile_y]
        hidden_cols = jax.vmap(lambda coord: columns(padded, coord, False))(own_coords)
        grad_pre = jax.vmap(lambda cols_one, cot_row, flag: forward_slot(cols_one, cot_row, flag, weight_flat))(
            hidden_cols, cot_grid[tile], occupied_grid[tile])
        weight_sum = weight_sum + lax.dot_general(grad_pre.astype(jnp.float32), hidden_cols.astype(jnp.float32),
                                                  (((0, 2), (0, 2)), ((), ())), precision=lax.Precision.HIGHEST)
        return weight_sum, grad_pre

    weight_grad, grad_pre_all = lax.scan(first_pass, jnp.zeros((CH, 27 * CH), jnp.float32), tile_ids)
    pre_grid = grad_pre_all.reshape(N_GX, N_GY, NB, CH, 512)

    def second_pass(tile):
        tile_x = tile // N_GY
        tile_y = tile % N_GY
        padded = tile_frame(pre_grid, coord_grid, tile_x, tile_y)
        gradient_columns = jax.vmap(lambda coord: columns(padded, coord, True))(coord_grid[tile_x, tile_y])
        backprop_total = jnp.einsum('iw,uwm->uim', weight_flipped.astype(jnp.float32), gradient_columns.astype(jnp.float32),
                                    precision=lax.Precision.HIGHEST)
        return (backprop_total * occupied_grid[tile][:, None, None]).astype(jnp.bfloat16)

    grad_skip = lax.map(second_pass, tile_ids)
    grad_coarse = jax.vmap(lambda grad_rows, parent_ids, tile_octants: coarse_gradient(grad_rows, parent_ids, tile_octants, NC, up_rows))(
        grad_skip, parents.reshape(tile_count, NB), octants.reshape(tile_count, NB, 3))
    return (grad_skip.reshape(tile_count * NB, CH, 512), grad_coarse.reshape(tile_count * NC, CH, 512),
            weight_grad.reshape(CH, 27, CH))
```

```python
import functools

import jax
import jax.numpy as jnp
from jax import lax
from jax.experimental import pallas as pl
from jax.experimental.pallas import tpu as pltpu
from jax.sharding import PartitionSpec as P

FB_X = 2
FB_Y = 2
MESH = pl.DeviceIdType.MESH
BF = jnp.bfloat16
F32 = jnp.float32
DIRS = ((-1, 0), (1, 0), (0, -1), (0, 1), (-1, -1), (-1, 1), (1, -1), (1, 1))
OPPOSITE = tuple(DIRS.index((-dx, -dy)) for dx, dy in DIRS)
NT = (((1,), (1,)), ((), ()))


def dot(a, b, dims=(((1,), (0,)), ((), ()))):
    return lax.dot_general(a, b, dims, preferred_element_type=F32)


def iota(shape, dim):
    return lax.broadcasted_iota(jnp.int32, shape, dim)


def one_hot(cond):
    return jnp.where(cond, 1.0, 0.0).astype(BF)


def identity(n):
    return one_hot(iota((n, n), 0) == iota((n, n), 1))


def child_row(v):
    p, q, s = v >> 6, (v >> 3) & 7, v & 7
    k = 4 * (p & 1) + 2 * (q & 1) + (s & 1)
    return k * 64 + (p >> 1) * 16 + (q >> 1) * 4 + (s >> 1)


def octant_column(u, meta, m):
    return (
        64 * (4 * meta[m, 3] + (u >> 4))
        + 8 * (4 * meta[m, 4] + ((u >> 2) & 3))
        + 4 * meta[m, 5]
        + (u & 3)
    )


def padded_rows(block, width):
    extra = width - block.shape[0]
    if extra == 0:
        return block
    return jnp.concatenate([block, jnp.zeros((extra, block.shape[1]), block.dtype)], 0)


class Exchange:
    def __init__(self, sizes, face_send, face_recv, edge_send, edge_recv, send_sem, recv_sem):
        gx, gy = lax.axis_index("gx"), lax.axis_index("gy")
        nx, ny = sizes
        self.refs = (face_send, face_recv, edge_send, edge_recv)
        self.sems = (send_sem, recv_sem)
        self.there, self.target = [], []
        for dx, dy in DIRS:
            x, y = gx + dx, gy + dy
            self.there.append((x >= 0) & (x < nx) & (y >= 0) & (y < ny))
            self.target.append((x, y))

    def greet(self):
        barrier = pltpu.get_barrier_semaphore()
        for d in range(8):
            @pl.when(self.there[d])
            def _():
                pl.semaphore_signal(barrier, inc=1, device_id=self.target[d], device_id_type=MESH)

    def await_greetings(self):
        peers = sum(there.astype(jnp.int32) for there in self.there)
        pl.semaphore_wait(pltpu.get_barrier_semaphore(), peers)

    def copy(self, d, landing):
        face_send, face_recv, edge_send, edge_recv = self.refs
        send, recv = (face_send, face_recv) if d < 4 else (edge_send, edge_recv)
        return pltpu.make_async_remote_copy(
            src_ref=send.at[d % 4],
            dst_ref=recv.at[landing % 4],
            send_sem=self.sems[0].at[d],
            recv_sem=self.sems[1].at[landing],
            device_id=self.target[d],
            device_id_type=MESH,
        )

    def pack(self, own, info):
        face_send, face_recv, edge_send, edge_recv = self.refs
        for d, (dx, dy) in enumerate(DIRS):
            x = 7 if dx > 0 else 0
            y = 7 if dy > 0 else 0
            if d < 2:
                face_send[d, 0:8] = own[8 * x : 8 * x + 8]
            elif d < 4:
                for i in range(8):
                    face_send[d, i] = own[8 * i + y]
            else:
                edge_send[d - 4, 0] = own[8 * x + y]
            if d < 4:
                face_send[d, 8:11] = info[...]
            else:
                edge_send[d - 4, 1:4] = info[...]

    def start(self):
        _, face_recv, _, edge_recv = self.refs
        for d in range(8):
            @pl.when(self.there[d])
            def _():
                self.copy(d, OPPOSITE[d]).start()

            @pl.when(jnp.logical_not(self.there[d]))
            def _():
                recv = face_recv if d < 4 else edge_recv
                recv[d % 4] = jnp.zeros(recv.shape[1:], recv.dtype)

    def finish(self):
        for d in range(8):
            @pl.when(self.there[d])
            def _():
                copy = self.copy(d, d)
                copy.wait_send()
                copy.wait_recv()


def weights_of(place, meta, m, dx, dy):
    x, y, z = place
    base = [meta[m, i].astype(F32) for i in range(3)]
    same = (x == base[0] + float(dx)) & (y == base[1] + float(dy))
    step = z - base[2]
    here = jnp.where(same & (step == 0.0), 1.0, 0.0)
    below = jnp.where(same & (step == -1.0), 1.0, 0.0)
    above = jnp.where(same & (step == 1.0), 1.0, 0.0)
    level = iota(here.shape, 0)
    return jnp.where(level == 0, below, here), here, jnp.where(level == 7, above, here)


def shifted(block):
    width = block.shape[-1]
    flat = block.reshape(-1, 8, width)
    down = pltpu.roll(flat, 1, 1).reshape(block.shape)
    up = pltpu.roll(flat, 7, 1).reshape(block.shape)
    return down, block, up


def sum_sources(sources):
    total = None
    for block, weights in sources:
        terms = [part * weight for part, weight in zip(shifted(block), weights)]
        total = terms if total is None else [a + b for a, b in zip(total, terms)]
    return total


def put(window, at_x, at_y, per_slot):
    width = per_slot[0][0].shape[-1]
    for k in range(3):
        both = jnp.concatenate([parts[k] for parts in per_slot], 1).astype(BF)
        rows = both.shape[0]
        if at_x is None:
            for i in range(rows):
                window[i + 1, at_y, :, k * width : (k + 1) * width] = both[i]
        elif at_y is None:
            window[at_x, 1 : 1 + rows, :, k * width : (k + 1) * width] = both
        else:
            window[at_x, at_y, :, k * width : (k + 1) * width] = both[0]


def own_place(meta, s, width):
    return [jnp.full((8, width), meta[s, i].astype(F32), F32) for i in range(3)]


def build_centre(window, own, meta, slots):
    width = own.shape[-1]
    ones = jnp.ones((8, width), F32)
    level = iota((8, width), 0)
    self_weights = (jnp.where(level == 0, 0.0, ones), ones, jnp.where(level == 7, 0.0, ones))
    other = [
        [(s, weights_of(own_place(meta, s, width), meta, m, 0, 0)) for s in range(slots) if s != m]
        for m in range(slots)
    ]

    def step(x, carry):
        rows = own[pl.ds(8 * x, 8)].astype(F32)
        blocks = [rows[:, 8 * s : 8 * s + 8] for s in range(slots)]
        per_slot = []
        for m in range(slots):
            sources = [(blocks[m], self_weights)] + [(blocks[s], w) for s, w in other[m]]
            per_slot.append(sum_sources(sources))
        put(window, x + 1, None, per_slot)
        return carry

    lax.fori_loop(0, 8, step, 0)


def build_border(window, own, face_recv, edge_recv, meta, slots):
    width = own.shape[-1]
    for dx, dy in DIRS:
        x = {-1: 7, 0: None, 1: 0}[dx]
        y = {-1: 7, 0: None, 1: 0}[dy]
        if dx and dy:
            own_rows = own[8 * x + y][None]
        elif dx:
            own_rows = own[8 * x : 8 * x + 8]
        else:
            own_rows = jnp.stack([own[8 * i + y] for i in range(8)], 0)
        own_rows = own_rows.astype(F32)
        tiles = []
        if dx:
            ref, d = face_recv, DIRS.index((dx, 0))
            rows = ref[d, y : y + 1] if dy else ref[d, 0:8]
            tiles.append((rows, ref[d, 8:11], dx, 0))
        if dy:
            ref, d = face_recv, DIRS.index((0, dy))
            rows = ref[d, x : x + 1] if dx else ref[d, 0:8]
            tiles.append((rows, ref[d, 8:11], 0, dy))
        if dx and dy:
            d = DIRS.index((dx, dy)) - 4
            tiles.append((edge_recv[d, 0:1], edge_recv[d, 1:4], dx, dy))
        tiles = [(rows.astype(F32), info.astype(F32), tx, ty) for rows, info, tx, ty in tiles]
        per_slot = []
        for m in range(slots):
            sources = []
            for s in range(slots):
                span = slice(8 * s, 8 * s + 8)
                if s != m:
                    place = own_place(meta, s, width)
                    sources.append((own_rows[:, span], weights_of(place, meta, m, dx, dy)))
                for rows, info, tx, ty in tiles:
                    place = (
                        info[0, span] + float(FB_X * tx),
                        info[1, span] + float(FB_Y * ty),
                        info[2, span],
                    )
                    sources.append((rows[:, span], weights_of(place, meta, m, dx, dy)))
            per_slot.append(sum_sources(sources))
        put(
            window,
            None if not dx else (0 if dx < 0 else 9),
            None if not dy else (0 if dy < 0 else 9),
            per_slot,
        )


def patch(window, j):
    x, y = j // 3, j % 3
    view = window[pl.ds(x, 8), pl.ds(y, 8)]
    return view.reshape(64 * view.shape[2], view.shape[3])


def forward_kernel(
    sizes, meta, info, skip, coarse, cot, up, weight, grad_pre, grad_weight,
    own, window, acc, turned, face_send, face_recv, edge_send, edge_recv, send_sem, recv_sem,
):
    slots, channels, voxels = skip.shape
    width = own.shape[-1]
    exchange = Exchange(sizes, face_send, face_recv, edge_send, edge_recv, send_sem, recv_sem)
    exchange.greet()
    eye = identity(voxels)
    spread = one_hot(
        iota((voxels, voxels), 1) == child_row(iota((voxels, voxels), 0))
    )
    rows = []
    for m in range(slots):
        octant = None
        column = octant_column(iota((64, voxels), 0), meta, m)
        for n in range(coarse.shape[0]):
            pick = one_hot((iota((64, voxels), 1) == column) & (meta[m, 6] == n))
            part = dot(pick, padded_rows(coarse[n], width), NT)
            octant = part if octant is None else octant + part
        lifted = dot(octant.astype(BF), up[...], NT)
        lifted = jnp.concatenate([lifted[:, k * width : (k + 1) * width] for k in range(8)], 0)
        high = lifted.astype(BF)
        low = (lifted - high.astype(F32)).astype(BF)
        total = dot(spread, high) + dot(spread, low) + dot(eye, padded_rows(skip[m], width), NT)
        rows.append((total * meta[m, 7].astype(F32)).reshape(64, 8, width))
    own[...] = jnp.concatenate(rows, 1).astype(BF)
    exchange.pack(own, info)
    exchange.await_greetings()
    exchange.start()
    build_centre(window, own, meta, slots)
    exchange.finish()
    build_border(window, own, face_recv, edge_recv, meta, slots)
    acc[...] = jnp.zeros_like(acc)

    def conv(j, carry):
        acc[...] += dot(patch(window, j), weight[j], NT)
        return carry

    lax.fori_loop(0, 9, conv, 0)
    pre_all = acc[...].reshape(64, 8 * slots, width)
    grads = []
    for m in range(slots):
        pre = pre_all[:, 8 * m : 8 * m + 8].reshape(voxels, width)
        sigma = 1.0 / (1.0 + jnp.exp(-pre))
        value = dot(eye, padded_rows(cot[m], width), NT)
        value = value * (sigma * (1.0 + pre * (1.0 - sigma))) * meta[m, 7].astype(F32)
        grads.append(value.reshape(64, 8, width))
    grad = jnp.concatenate(grads, 1)
    grad_pre[...] = grad.astype(BF)
    turned[...] = jnp.transpose(grad.reshape(64 * 8 * slots, width)).astype(BF)

    def outer(j, carry):
        grad_weight[j] = dot(turned[...], patch(window, j)).astype(BF)
        return carry

    lax.fori_loop(0, 9, outer, 0)


def backward_kernel(
    sizes, meta, info, own, up, weight, grad_skip, grad_coarse,
    window, acc, face_send, face_recv, edge_send, edge_recv, send_sem, recv_sem,
):
    slots, channels, voxels = grad_skip.shape
    width = own.shape[-1]
    exchange = Exchange(sizes, face_send, face_recv, edge_send, edge_recv, send_sem, recv_sem)
    exchange.greet()
    exchange.pack(own, info)
    exchange.await_greetings()
    exchange.start()
    build_centre(window, own, meta, slots)
    exchange.finish()
    build_border(window, own, face_recv, edge_recv, meta, slots)
    acc[...] = jnp.zeros_like(acc)

    def conv(j, carry):
        acc[...] += dot(patch(window, j), weight[j])
        return carry

    lax.fori_loop(0, 9, conv, 0)
    all_rows = acc[...].reshape(64, 8 * slots, width)
    gather = one_hot(iota((voxels, voxels), 0) == child_row(iota((voxels, voxels), 1)))
    folded = []
    for m in range(slots):
        rows = all_rows[:, 8 * m : 8 * m + 8].reshape(voxels, width) * meta[m, 7].astype(F32)
        grad_skip[m] = jnp.transpose(rows).astype(BF)[:channels]
        grouped = dot(gather, rows.astype(BF)).astype(BF)
        grouped = jnp.concatenate([grouped[64 * k : 64 * k + 64] for k in range(8)], 1)
        folded.append(jnp.transpose(dot(grouped, up[...])).astype(BF))
    for n in range(grad_coarse.shape[0]):
        total = None
        for m in range(slots):
            column = octant_column(iota((64, voxels), 0), meta, m)
            place = one_hot((iota((64, voxels), 1) == column) & (meta[m, 6] == n))
            part = dot(folded[m], place)
            total = part if total is None else total + part
        grad_coarse[n] = total.astype(BF)[:channels]


def exchange_scratch(slots, width):
    return [
        pltpu.VMEM((4, 11, 8 * slots, width), BF),
        pltpu.VMEM((4, 11, 8 * slots, width), BF),
        pltpu.VMEM((4, 4, 8 * slots, width), BF),
        pltpu.VMEM((4, 4, 8 * slots, width), BF),
        pltpu.SemaphoreType.DMA((8,)),
        pltpu.SemaphoreType.DMA((8,)),
    ]


def local(
    sizes, skip_feature_rows, coarse_features, cotangent, fine_coords, coarse_coords,
    parents, counts, conv_weight, up_weight,
):
    slots, channels, voxels = skip_feature_rows.shape
    width = -(-channels // 128) * 128
    extra = width - channels
    octants = fine_coords - 2 * coarse_coords[parents]
    occupied = (jnp.arange(slots, dtype=jnp.int32) < counts[0]).astype(jnp.int32)
    meta = jnp.concatenate([fine_coords, octants, parents[:, None], occupied[:, None]], 1)
    info = jnp.broadcast_to(
        jnp.repeat(fine_coords.T.astype(BF), 8, axis=1)[:, :, None], (3, 8 * slots, width)
    )
    up = jnp.pad(up_weight, ((0, 0), (0, extra), (0, extra))).reshape(8 * width, width)
    padded = jnp.pad(conv_weight, ((0, extra), (0, 0), (0, extra)))
    weight_forward = padded.reshape(width, 9, 3 * width).transpose(1, 0, 2)
    weight_backward = padded[:, ::-1].transpose(1, 0, 2).reshape(9, 3 * width, width)
    smem = pl.BlockSpec(memory_space=pltpu.SMEM)
    vmem = pl.BlockSpec(memory_space=pltpu.VMEM)
    window = pltpu.VMEM((10, 10, 8 * slots, 3 * width), BF)
    acc = pltpu.VMEM((64 * 8 * slots, width), F32)
    rows = jax.ShapeDtypeStruct((64, 8 * slots, width), BF)
    limit = 56 * 1024 * 1024
    flops = 2 * 27 * slots * voxels * channels * channels
    grad_pre, grad_weight = pl.pallas_call(
        functools.partial(forward_kernel, sizes),
        out_shape=(rows, jax.ShapeDtypeStruct((9, width, 3 * width), BF)),
        in_specs=[smem] + [vmem] * 6,
        out_specs=(vmem, vmem),
        scratch_shapes=[
            pltpu.VMEM(rows.shape, BF), window, acc,
            pltpu.VMEM((width, 64 * 8 * slots), BF),
        ] + exchange_scratch(slots, width),
        compiler_params=pltpu.CompilerParams(
            collective_id=0, has_side_effects=True, vmem_limit_bytes=limit
        ),
        cost_estimate=pl.CostEstimate(flops=2 * flops, bytes_accessed=12 << 20, transcendentals=0),
        name="forward",
    )(meta, info, skip_feature_rows, coarse_features, cotangent, up, weight_forward)
    grad_conv = grad_weight.reshape(9, width, 3, width)[:, :channels, :, :channels]
    grad_conv = grad_conv.transpose(1, 0, 2, 3).reshape(channels, 27 * channels)
    grad_conv = lax.psum_scatter(grad_conv, "gy", scatter_dimension=0, tiled=True)
    grad_conv = lax.psum(grad_conv, "gx").astype(F32)
    slab = jax.ShapeDtypeStruct((slots, channels, voxels), BF)
    coarse_slab = jax.ShapeDtypeStruct(coarse_features.shape, BF)
    grad_skip, grad_coarse = pl.pallas_call(
        functools.partial(backward_kernel, sizes),
        out_shape=(slab, coarse_slab),
        in_specs=[smem] + [vmem] * 4,
        out_specs=(vmem, vmem),
        scratch_shapes=[window, acc] + exchange_scratch(slots, width),
        compiler_params=pltpu.CompilerParams(
            collective_id=1, has_side_effects=True, vmem_limit_bytes=limit
        ),
        cost_estimate=pl.CostEstimate(flops=8 * flops, bytes_accessed=64 << 20, transcendentals=0),
        name="backward",
    )(meta, info, grad_pre, up, weight_backward)
    return (grad_skip, grad_coarse, grad_conv.reshape(grad_conv.shape[0], 27, channels))


def solution(mesh):
    in_specs = (
        P(("gx", "gy"), None, None),
        P(("gx", "gy"), None, None),
        P(("gx", "gy"), None, None),
        P(("gx", "gy"), None),
        P(("gx", "gy"), None),
        P(("gx", "gy")),
        P(("gx", "gy")),
        P(),
        P(),
    )
    out_specs = (P(("gx", "gy"), None, None), P(("gx", "gy"), None, None), P("gy", None, None))
    sizes = (mesh.shape["gx"], mesh.shape["gy"])
    return jax.shard_map(
        functools.partial(local, sizes),
        mesh=mesh,
        in_specs=in_specs,
        out_specs=out_specs,
        check_vma=False,
    )
```

```python
import functools

import jax
import jax.numpy as jnp
from jax import lax
from jax.experimental import pallas as pl
from jax.experimental.pallas import tpu as pltpu
from jax.sharding import PartitionSpec as P

FB_X = 2
FB_Y = 2
MESH = pl.DeviceIdType.MESH
BF = jnp.bfloat16
F32 = jnp.float32
DIRS = ((-1, 0), (1, 0), (0, -1), (0, 1), (-1, -1), (-1, 1), (1, -1), (1, 1))
OPPOSITE = tuple(DIRS.index((-dx, -dy)) for dx, dy in DIRS)
NT = (((1,), (1,)), ((), ()))


def dot(a, b, dims=(((1,), (0,)), ((), ()))):
    return lax.dot_general(a, b, dims, preferred_element_type=F32)


def iota(shape, dim):
    return lax.broadcasted_iota(jnp.int32, shape, dim)


def one_hot(cond):
    return jnp.where(cond, 1.0, 0.0).astype(BF)


def identity(n):
    return one_hot(iota((n, n), 0) == iota((n, n), 1))


def child_row(v):
    p, q, s = v >> 6, (v >> 3) & 7, v & 7
    k = 4 * (p & 1) + 2 * (q & 1) + (s & 1)
    return k * 64 + (p >> 1) * 16 + (q >> 1) * 4 + (s >> 1)


def octant_column(u, meta, m):
    return (
        64 * (4 * meta[m, 3] + (u >> 4))
        + 8 * (4 * meta[m, 4] + ((u >> 2) & 3))
        + 4 * meta[m, 5]
        + (u & 3)
    )


def padded_rows(block, width):
    extra = width - block.shape[0]
    if extra == 0:
        return block
    return jnp.concatenate([block, jnp.zeros((extra, block.shape[1]), block.dtype)], 0)


class Exchange:
    def __init__(self, sizes, face_send, face_recv, edge_send, edge_recv, send_sem, recv_sem):
        gx, gy = lax.axis_index("gx"), lax.axis_index("gy")
        nx, ny = sizes
        self.refs = (face_send, face_recv, edge_send, edge_recv)
        self.sems = (send_sem, recv_sem)
        self.there, self.target = [], []
        for dx, dy in DIRS:
            x, y = gx + dx, gy + dy
            self.there.append((x >= 0) & (x < nx) & (y >= 0) & (y < ny))
            self.target.append((x, y))

    def greet(self, others):
        barrier = pltpu.get_barrier_semaphore()
        for d in range(8):
            @pl.when(self.there[d])
            def _():
                pl.semaphore_signal(barrier, inc=1, device_id=self.target[d], device_id_type=MESH)

        for target in others:
            pl.semaphore_signal(barrier, inc=1, device_id=target, device_id_type=MESH)

    def await_greetings(self, others):
        peers = len(others) + sum(there.astype(jnp.int32) for there in self.there)
        pl.semaphore_wait(pltpu.get_barrier_semaphore(), peers)

    def copy(self, d, landing):
        face_send, face_recv, edge_send, edge_recv = self.refs
        send, recv = (face_send, face_recv) if d < 4 else (edge_send, edge_recv)
        return pltpu.make_async_remote_copy(
            src_ref=send.at[d % 4],
            dst_ref=recv.at[landing % 4],
            send_sem=self.sems[0].at[d],
            recv_sem=self.sems[1].at[landing],
            device_id=self.target[d],
            device_id_type=MESH,
        )

    def pack(self, own, info):
        face_send, face_recv, edge_send, edge_recv = self.refs
        for d, (dx, dy) in enumerate(DIRS):
            x = 7 if dx > 0 else 0
            y = 7 if dy > 0 else 0
            if d < 2:
                face_send[d, 0:8] = own[8 * x : 8 * x + 8]
            elif d < 4:
                for i in range(8):
                    face_send[d, i] = own[8 * i + y]
            else:
                edge_send[d - 4, 0] = own[8 * x + y]
            if d < 4:
                face_send[d, 8:11] = info
            else:
                edge_send[d - 4, 1:4] = info

    def start(self):
        _, face_recv, _, edge_recv = self.refs
        for d in range(8):
            @pl.when(self.there[d])
            def _():
                self.copy(d, OPPOSITE[d]).start()

            @pl.when(jnp.logical_not(self.there[d]))
            def _():
                recv = face_recv if d < 4 else edge_recv
                recv[d % 4] = jnp.zeros(recv.shape[1:], recv.dtype)

    def finish(self):
        for d in range(8):
            @pl.when(self.there[d])
            def _():
                copy = self.copy(d, d)
                copy.wait_send()
                copy.wait_recv()


def weights_of(place, meta, m, dx, dy):
    x, y, z = place
    base = [meta[m, i].astype(F32) for i in range(3)]
    same = (x == base[0] + float(dx)) & (y == base[1] + float(dy))
    step = z - base[2]
    here = jnp.where(same & (step == 0.0), 1.0, 0.0)
    below = jnp.where(same & (step == -1.0), 1.0, 0.0)
    above = jnp.where(same & (step == 1.0), 1.0, 0.0)
    level = iota(here.shape, 0)
    return jnp.where(level == 0, below, here), here, jnp.where(level == 7, above, here)


def shifted(block):
    width = block.shape[-1]
    flat = block.reshape(-1, 8, width)
    down = pltpu.roll(flat, 1, 1).reshape(block.shape)
    up = pltpu.roll(flat, 7, 1).reshape(block.shape)
    return down, block, up


def sum_sources(sources):
    total = None
    for block, weights in sources:
        terms = [part * weight for part, weight in zip(shifted(block), weights)]
        total = terms if total is None else [a + b for a, b in zip(total, terms)]
    return total


def put(window, at_x, at_y, per_slot):
    width = per_slot[0][0].shape[-1]
    for k in range(3):
        both = jnp.concatenate([parts[k] for parts in per_slot], 1).astype(BF)
        rows = both.shape[0]
        if at_x is None:
            for i in range(rows):
                window[i + 1, at_y, :, k * width : (k + 1) * width] = both[i]
        elif at_y is None:
            window[at_x, 1 : 1 + rows, :, k * width : (k + 1) * width] = both
        else:
            window[at_x, at_y, :, k * width : (k + 1) * width] = both[0]


def own_place(meta, s, width):
    return [jnp.full((8, width), meta[s, i].astype(F32), F32) for i in range(3)]


def build_centre(window, own, meta, slots):
    width = own.shape[-1]
    ones = jnp.ones((8, width), F32)
    level = iota((8, width), 0)
    self_weights = (jnp.where(level == 0, 0.0, ones), ones, jnp.where(level == 7, 0.0, ones))
    other = [
        [(s, weights_of(own_place(meta, s, width), meta, m, 0, 0)) for s in range(slots) if s != m]
        for m in range(slots)
    ]

    def step(x, carry):
        rows = own[pl.ds(8 * x, 8)].astype(F32)
        blocks = [rows[:, 8 * s : 8 * s + 8] for s in range(slots)]
        per_slot = []
        for m in range(slots):
            sources = [(blocks[m], self_weights)] + [(blocks[s], w) for s, w in other[m]]
            per_slot.append(sum_sources(sources))
        put(window, x + 1, None, per_slot)
        return carry

    lax.fori_loop(0, 8, step, 0)


def build_border(window, own, face_recv, edge_recv, meta, slots):
    width = own.shape[-1]
    for dx, dy in DIRS:
        x = {-1: 7, 0: None, 1: 0}[dx]
        y = {-1: 7, 0: None, 1: 0}[dy]
        if dx and dy:
            own_rows = own[8 * x + y][None]
        elif dx:
            own_rows = own[8 * x : 8 * x + 8]
        else:
            own_rows = jnp.stack([own[8 * i + y] for i in range(8)], 0)
        own_rows = own_rows.astype(F32)
        tiles = []
        if dx:
            ref, d = face_recv, DIRS.index((dx, 0))
            rows = ref[d, y : y + 1] if dy else ref[d, 0:8]
            tiles.append((rows, ref[d, 8:11], dx, 0))
        if dy:
            ref, d = face_recv, DIRS.index((0, dy))
            rows = ref[d, x : x + 1] if dx else ref[d, 0:8]
            tiles.append((rows, ref[d, 8:11], 0, dy))
        if dx and dy:
            d = DIRS.index((dx, dy)) - 4
            tiles.append((edge_recv[d, 0:1], edge_recv[d, 1:4], dx, dy))
        tiles = [(rows.astype(F32), info.astype(F32), tx, ty) for rows, info, tx, ty in tiles]
        per_slot = []
        for m in range(slots):
            sources = []
            for s in range(slots):
                span = slice(8 * s, 8 * s + 8)
                if s != m:
                    place = own_place(meta, s, width)
                    sources.append((own_rows[:, span], weights_of(place, meta, m, dx, dy)))
                for rows, info, tx, ty in tiles:
                    place = (
                        info[0, span] + float(FB_X * tx),
                        info[1, span] + float(FB_Y * ty),
                        info[2, span],
                    )
                    sources.append((rows[:, span], weights_of(place, meta, m, dx, dy)))
            per_slot.append(sum_sources(sources))
        put(
            window,
            None if not dx else (0 if dx < 0 else 9),
            None if not dy else (0 if dy < 0 else 9),
            per_slot,
        )


def patch(window, j):
    x, y = j // 3, j % 3
    view = window[pl.ds(x, 8), pl.ds(y, 8)]
    return view.reshape(64 * view.shape[2], view.shape[3])


class Ring:
    def __init__(self, index, count, target, send_sem, recv_sem):
        self.index, self.count = index, count
        self.sems = (send_sem, recv_sem)
        self.ranks = [lax.rem(index + r, count) for r in range(1, count)]
        self.origins = [lax.rem(index + count - r, count) for r in range(1, count)]
        self.targets = [target(rank) for rank in self.ranks]

    def copies(self, source, landing):
        return [
            pltpu.make_async_remote_copy(
                src_ref=source(i, self.ranks[i]),
                dst_ref=landing(i, self.index),
                send_sem=self.sems[0].at[i],
                recv_sem=self.sems[1].at[i],
                device_id=self.targets[i],
                device_id_type=MESH,
            )
            for i in range(self.count - 1)
        ]

    def start(self, source, landing):
        for copy in self.copies(source, landing):
            copy.start()

    def finish(self, source, arrived):
        sends = self.copies(source, arrived)
        for i, copy in enumerate(sends):
            copy.wait_send()
            pltpu.make_async_remote_copy(
                src_ref=source(i, self.ranks[i]),
                dst_ref=arrived(i, self.origins[i]),
                send_sem=self.sems[0].at[i],
                recv_sem=self.sems[1].at[i],
                device_id=self.targets[i],
                device_id_type=MESH,
            ).wait_recv()


def add_rows(target, own, arrived, count, rows, step):
    def body(i, carry):
        at = pl.multiple_of(i * step, step)
        total = own(at).astype(F32)
        for r in range(count):
            total = total + arrived[r, pl.ds(at, step)].astype(F32)
        target(at, total.astype(BF))
        return carry

    lax.fori_loop(0, rows // step, body, 0)


class Plan:
    def __init__(self, sizes, channels):
        self.nx, self.ny = sizes
        self.inner = 4 if self.nx % 4 == 0 else 1
        self.outer = self.nx // self.inner
        self.rows = channels // self.ny
        self.padded = -(-self.rows // 16) * 16
        self.full = channels // 128
        self.tail = channels % 128
        self.per = 128 // self.tail if self.tail else 1
        self.groups = -(-27 // self.per) if self.tail else 0
        total = (27 * self.full + self.groups) * self.padded
        self.chunk = -(-total // (16 * self.nx)) * 16
        self.total = self.chunk * self.nx
        self.used = total


def pack_weight_gradient(plan, stage, wide, width):
    rows, padded = plan.rows, plan.padded

    def piece(e, share, low, high):
        j, k = e // 3, e % 3
        value = wide[j, share * rows : (share + 1) * rows, k * width + low : k * width + high]
        if padded != rows:
            value = jnp.concatenate([value, jnp.zeros((padded - rows, high - low), F32)], 0)
        return value

    for share in range(plan.ny):
        at = 0
        for e in range(27):
            for tile in range(plan.full):
                block = piece(e, share, 128 * tile, 128 * tile + 128)
                stage[share, at : at + padded] = block.astype(BF)
                at += padded
        for g in range(plan.groups):
            parts = []
            for e in range(g * plan.per, (g + 1) * plan.per):
                low = 128 * plan.full
                parts.append(
                    piece(e, share, low, low + plan.tail)
                    if e < 27
                    else jnp.zeros((padded, plan.tail), F32)
                )
            stage[share, at : at + padded] = jnp.concatenate(parts, 1).astype(BF)
            at += padded
        if at < plan.total:
            stage[share, at:] = jnp.zeros((plan.total - at, 128), BF)


def unpack_weight_gradient(plan, final, out):
    rows, padded, tail = plan.rows, plan.padded, plan.tail
    at = 0
    for e in range(27):
        for tile in range(plan.full):
            out[e, :, 128 * tile : 128 * tile + 128] = final[at : at + padded].astype(F32)[:rows]
            at += padded
    for g in range(plan.groups):
        block = final[at : at + padded].astype(F32)[:rows]
        for i, e in enumerate(range(g * plan.per, min(27, (g + 1) * plan.per))):
            out[e, :, 128 * plan.full :] = block[:, i * tail : (i + 1) * tail]
        at += padded


def whole_kernel(
    sizes, plan, fine, coarse_place, parents, counts, skip, coarse, cot, up_raw, weight_raw,
    grad_skip, grad_coarse, grad_conv,
    own, window, acc, turned, up, weight, wide, stage, summed, partial, final,
    in_y, in_inner, in_outer,
    face_send, face_recv, edge_send, edge_recv, send_sem, recv_sem,
    face_send2, face_recv2, edge_send2, edge_recv2, send_sem2, recv_sem2,
    ring_send, ring_recv,
):
    slots, channels, voxels = skip.shape
    width = own.shape[-1]
    gx, gy = lax.axis_index("gx"), lax.axis_index("gy")
    first = Exchange(sizes, face_send, face_recv, edge_send, edge_recv, send_sem, recv_sem)
    second = Exchange(sizes, face_send2, face_recv2, edge_send2, edge_recv2, send_sem2, recv_sem2)
    inner, outer = plan.inner, plan.outer
    a, b = lax.rem(gx, inner), lax.div(gx, inner)

    def sems(i):
        return ring_send.at[i], ring_recv.at[i]

    ring_y = Ring(gy, plan.ny, lambda r: (gx, r), *sems(0))
    to_inner = lambda r: (b * inner + r, gy)
    to_outer = lambda r: (r * inner + a, gy)
    ring_1 = Ring(a, inner, to_inner, *sems(1))
    ring_2 = Ring(b, outer, to_outer, *sems(2))
    ring_3 = Ring(b, outer, to_outer, *sems(3))
    ring_4 = Ring(a, inner, to_inner, *sems(4))
    others = ring_y.targets + ring_1.targets + ring_2.targets
    first.greet(others)

    meta = {}
    for m in range(slots):
        parent = parents[m]
        for i in range(3):
            base = sum(
                jnp.where(parent == n, coarse_place[n, i], 0) for n in range(coarse.shape[0])
            )
            meta[m, i] = fine[m, i]
            meta[m, 3 + i] = fine[m, i] - 2 * base
        meta[m, 6] = parent
        meta[m, 7] = jnp.where(m < counts[0], 1, 0)
    info = jnp.stack(
        [
            jnp.concatenate(
                [jnp.full((8, width), meta[m, i].astype(F32), F32) for m in range(slots)], 0
            )
            for i in range(3)
        ],
        0,
    ).astype(BF)

    up[...] = jnp.zeros_like(up)
    for k in range(8):
        up[k * width : k * width + channels, 0:channels] = up_raw[k]
    weight[...] = jnp.zeros_like(weight)
    for e in range(27):
        low = (e % 3) * width
        weight[e // 3, 0:channels, low : low + channels] = weight_raw[e]

    eye = identity(voxels)
    spread = one_hot(iota((voxels, voxels), 1) == child_row(iota((voxels, voxels), 0)))
    rows = []
    for m in range(slots):
        octant = None
        column = octant_column(iota((64, voxels), 0), meta, m)
        for n in range(coarse.shape[0]):
            pick = one_hot((iota((64, voxels), 1) == column) & (meta[m, 6] == n))
            part = dot(pick, padded_rows(coarse[n], width), NT)
            octant = part if octant is None else octant + part
        lifted = dot(octant.astype(BF), up[...], NT)
        lifted = jnp.concatenate([lifted[:, k * width : (k + 1) * width] for k in range(8)], 0)
        high = lifted.astype(BF)
        low = (lifted - high.astype(F32)).astype(BF)
        total = dot(spread, high) + dot(spread, low) + dot(eye, padded_rows(skip[m], width), NT)
        rows.append((total * meta[m, 7].astype(F32)).reshape(64, 8, width))
    own[...] = jnp.concatenate(rows, 1).astype(BF)
    first.pack(own, info)
    first.await_greetings(others)
    first.start()
    build_centre(window, own, meta, slots)
    first.finish()
    build_border(window, own, face_recv, edge_recv, meta, slots)
    acc[...] = jnp.zeros_like(acc)

    def conv(j, carry):
        acc[...] += dot(patch(window, j), weight[j], NT)
        return carry

    lax.fori_loop(0, 9, conv, 0)
    pre_all = acc[...].reshape(64, 8 * slots, width)
    grads = []
    for m in range(slots):
        pre = pre_all[:, 8 * m : 8 * m + 8].reshape(voxels, width)
        sigma = 1.0 / (1.0 + jnp.exp(-pre))
        value = dot(eye, padded_rows(cot[m], width), NT)
        value = value * (sigma * (1.0 + pre * (1.0 - sigma))) * meta[m, 7].astype(F32)
        grads.append(value.reshape(64, 8, width))
    grad = jnp.concatenate(grads, 1)
    own[...] = grad.astype(BF)
    second.pack(own, info)
    second.start()
    turned[...] = jnp.transpose(grad.reshape(64 * 8 * slots, width)).astype(BF)

    def outer_product(j, carry):
        wide[j] = dot(turned[...], patch(window, j))
        return carry

    lax.fori_loop(0, 9, outer_product, 0)
    pack_weight_gradient(plan, stage, wide, width)

    chunk, total, part = plan.chunk, plan.total, plan.chunk * outer
    span_1 = lambda r: pl.ds(pl.multiple_of(r * part, 16), part)
    span_2 = lambda r: pl.ds(pl.multiple_of(r * chunk, 16), chunk)
    span_f = lambda ra, rb: pl.ds(pl.multiple_of((ra * outer + rb) * chunk, 16), chunk)
    source_y, land_y = (lambda i, r: stage.at[r]), (lambda i, r: in_y.at[i])
    source_1, land_1 = (lambda i, r: summed.at[span_1(r)]), (lambda i, r: in_inner.at[i])
    source_2, land_2 = (lambda i, r: partial.at[span_2(r)]), (lambda i, r: in_outer.at[i])
    source_3, land_3 = (lambda i, r: final.at[span_f(a, b)]), (lambda i, r: final.at[span_f(a, r)])
    source_4, land_4 = (lambda i, r: final.at[span_1(a)]), (lambda i, r: final.at[span_1(r)])

    def store_to(ref, base):
        def store(at, value):
            ref[pl.ds(pl.multiple_of(base + at, 16), value.shape[0])] = value
        return store

    def load_from(ref, base, step):
        return lambda at: ref[pl.ds(pl.multiple_of(base + at, 16), step)]

    ring_y.start(source_y, land_y)
    build_centre(window, own, meta, slots)
    ring_y.finish(source_y, land_y)
    add_rows(
        store_to(summed, 0), lambda at: stage[gy, pl.ds(at, chunk)], in_y, plan.ny - 1, total, chunk
    )
    ring_1.start(source_1, land_1)

    second.finish()
    build_border(window, own, face_recv2, edge_recv2, meta, slots)
    acc[...] = jnp.zeros_like(acc)

    def conv_back(j, carry):
        rows = patch(window, j)
        value = None
        for k in range(3):
            term = dot(
                rows[:, k * width : (k + 1) * width],
                weight[8 - j, :, (2 - k) * width : (3 - k) * width],
            )
            value = term if value is None else value + term
        acc[...] += value
        return carry

    lax.fori_loop(0, 9, conv_back, 0)
    ring_1.finish(source_1, land_1)
    add_rows(
        store_to(partial, 0), load_from(summed, a * part, chunk), in_inner, inner - 1, part, chunk
    )
    ring_2.start(source_2, land_2)

    all_rows = acc[...].reshape(64, 8 * slots, width)
    gather = one_hot(iota((voxels, voxels), 0) == child_row(iota((voxels, voxels), 1)))
    folded = []
    for m in range(slots):
        rows = all_rows[:, 8 * m : 8 * m + 8].reshape(voxels, width) * meta[m, 7].astype(F32)
        grad_skip[m] = jnp.transpose(rows).astype(BF)[:channels]
        grouped = dot(gather, rows.astype(BF)).astype(BF)
        folded.append(jnp.concatenate([grouped[64 * k : 64 * k + 64] for k in range(8)], 1))

    ring_2.finish(source_2, land_2)
    add_rows(
        store_to(final, (a * outer + b) * chunk), load_from(partial, b * chunk, 16),
        in_outer, outer - 1, chunk, 16,
    )
    ring_3.start(source_3, land_3)
    folded = [jnp.transpose(dot(grouped, up[...])).astype(BF) for grouped in folded]
    ring_3.finish(source_3, land_3)
    ring_4.start(source_4, land_4)
    for n in range(grad_coarse.shape[0]):
        value = None
        for m in range(slots):
            column = octant_column(iota((64, voxels), 0), meta, m)
            place = one_hot((iota((64, voxels), 1) == column) & (meta[m, 6] == n))
            term = dot(folded[m], place)
            value = term if value is None else value + term
        grad_coarse[n] = value.astype(BF)[:channels]
    ring_4.finish(source_4, land_4)
    unpack_weight_gradient(plan, final, grad_conv)


def exchange_scratch(slots, width):
    return [
        pltpu.VMEM((4, 11, 8 * slots, width), BF),
        pltpu.VMEM((4, 11, 8 * slots, width), BF),
        pltpu.VMEM((4, 4, 8 * slots, width), BF),
        pltpu.VMEM((4, 4, 8 * slots, width), BF),
        pltpu.SemaphoreType.DMA((8,)),
        pltpu.SemaphoreType.DMA((8,)),
    ]


def local(
    sizes, skip_feature_rows, coarse_features, cotangent, fine_coords, coarse_coords,
    parents, counts, conv_weight, up_weight,
):
    slots, channels, voxels = skip_feature_rows.shape
    width = -(-channels // 128) * 128
    plan = Plan(sizes, channels)
    peers = max(plan.ny, plan.inner, plan.outer, 2) - 1
    smem = pl.BlockSpec(memory_space=pltpu.SMEM)
    vmem = pl.BlockSpec(memory_space=pltpu.VMEM)
    cells = 64 * 8 * slots
    grad_skip, grad_coarse, grad_conv = pl.pallas_call(
        functools.partial(whole_kernel, sizes, plan),
        out_shape=(
            jax.ShapeDtypeStruct((slots, channels, voxels), BF),
            jax.ShapeDtypeStruct(coarse_features.shape, BF),
            jax.ShapeDtypeStruct((27, plan.rows, channels), F32),
        ),
        in_specs=[smem] * 4 + [vmem] * 5,
        out_specs=(vmem, vmem, vmem),
        scratch_shapes=[
            pltpu.VMEM((64, 8 * slots, width), BF),
            pltpu.VMEM((10, 10, 8 * slots, 3 * width), BF),
            pltpu.VMEM((cells, width), F32),
            pltpu.VMEM((width, cells), BF),
            pltpu.VMEM((8 * width, width), BF),
            pltpu.VMEM((9, width, 3 * width), BF),
            pltpu.VMEM((9, width, 3 * width), F32),
            pltpu.VMEM((plan.ny, plan.total, 128), BF),
            pltpu.VMEM((plan.total, 128), BF),
            pltpu.VMEM((plan.chunk * plan.outer, 128), BF),
            pltpu.VMEM((plan.total, 128), BF),
            pltpu.VMEM((max(plan.ny - 1, 1), plan.total, 128), BF),
            pltpu.VMEM((max(plan.inner - 1, 1), plan.chunk * plan.outer, 128), BF),
            pltpu.VMEM((max(plan.outer - 1, 1), plan.chunk, 128), BF),
        ]
        + exchange_scratch(slots, width)
        + exchange_scratch(slots, width)
        + [pltpu.SemaphoreType.DMA((5, peers)), pltpu.SemaphoreType.DMA((5, peers))],
        compiler_params=pltpu.CompilerParams(
            collective_id=0, has_side_effects=True, vmem_limit_bytes=58 * 1024 * 1024
        ),
        cost_estimate=pl.CostEstimate(
            flops=6 * 27 * slots * voxels * channels * channels,
            bytes_accessed=12 << 20, transcendentals=0,
        ),
        name="whole",
    )(
        fine_coords, coarse_coords, parents, counts,
        skip_feature_rows, coarse_features, cotangent, up_weight,
        conv_weight.transpose(1, 0, 2),
    )
    return (grad_skip, grad_coarse, grad_conv.transpose(1, 0, 2))


def solution(mesh):
    in_specs = (
        P(("gx", "gy"), None, None),
        P(("gx", "gy"), None, None),
        P(("gx", "gy"), None, None),
        P(("gx", "gy"), None),
        P(("gx", "gy"), None),
        P(("gx", "gy")),
        P(("gx", "gy")),
        P(),
        P(),
    )
    out_specs = (P(("gx", "gy"), None, None), P(("gx", "gy"), None, None), P("gy", None, None))
    sizes = (mesh.shape["gx"], mesh.shape["gy"])
    return jax.shard_map(
        functools.partial(local, sizes),
        mesh=mesh,
        in_specs=in_specs,
        out_specs=out_specs,
        check_vma=False,
    )
```

```python
import functools

import jax
import jax.numpy as jnp
from jax import lax
from jax.experimental import pallas as pl
from jax.experimental.pallas import tpu as pltpu
from jax.sharding import PartitionSpec as P

FB_X = 2
FB_Y = 2
MESH = pl.DeviceIdType.MESH
BF = jnp.bfloat16
F32 = jnp.float32
DIRS = ((-1, 0), (1, 0), (0, -1), (0, 1), (-1, -1), (-1, 1), (1, -1), (1, 1))
OPPOSITE = tuple(DIRS.index((-dx, -dy)) for dx, dy in DIRS)
NT = (((1,), (1,)), ((), ()))


def dot(a, b, dims=(((1,), (0,)), ((), ()))):
    return lax.dot_general(a, b, dims, preferred_element_type=F32)


def iota(shape, dim):
    return lax.broadcasted_iota(jnp.int32, shape, dim)


def one_hot(cond):
    return jnp.where(cond, 1.0, 0.0).astype(BF)


def identity(n):
    return one_hot(iota((n, n), 0) == iota((n, n), 1))


def child_row(v):
    p, q, s = v >> 6, (v >> 3) & 7, v & 7
    k = 4 * (p & 1) + 2 * (q & 1) + (s & 1)
    return k * 64 + (p >> 1) * 16 + (q >> 1) * 4 + (s >> 1)


def octant_column(u, meta, m):
    return (
        64 * (4 * meta[m, 3] + (u >> 4))
        + 8 * (4 * meta[m, 4] + ((u >> 2) & 3))
        + 4 * meta[m, 5]
        + (u & 3)
    )


def padded_rows(block, width):
    extra = width - block.shape[0]
    if extra == 0:
        return block
    return jnp.concatenate([block, jnp.zeros((extra, block.shape[1]), block.dtype)], 0)


class Exchange:
    def __init__(self, sizes, face_send, face_recv, edge_send, edge_recv, send_sem, recv_sem):
        gx, gy = lax.axis_index("gx"), lax.axis_index("gy")
        nx, ny = sizes
        self.refs = (face_send, face_recv, edge_send, edge_recv)
        self.sems = (send_sem, recv_sem)
        self.there, self.target = [], []
        for dx, dy in DIRS:
            x, y = gx + dx, gy + dy
            self.there.append((x >= 0) & (x < nx) & (y >= 0) & (y < ny))
            self.target.append((x, y))

    def greet(self, others):
        barrier = pltpu.get_barrier_semaphore()
        for d in range(8):
            @pl.when(self.there[d])
            def _():
                pl.semaphore_signal(barrier, inc=1, device_id=self.target[d], device_id_type=MESH)

        for target in others:
            pl.semaphore_signal(barrier, inc=1, device_id=target, device_id_type=MESH)

    def await_greetings(self, others):
        peers = len(others) + sum(there.astype(jnp.int32) for there in self.there)
        pl.semaphore_wait(pltpu.get_barrier_semaphore(), peers)

    def copy(self, d, landing):
        face_send, face_recv, edge_send, edge_recv = self.refs
        send, recv = (face_send, face_recv) if d < 4 else (edge_send, edge_recv)
        return pltpu.make_async_remote_copy(
            src_ref=send.at[d % 4],
            dst_ref=recv.at[landing % 4],
            send_sem=self.sems[0].at[d],
            recv_sem=self.sems[1].at[landing],
            device_id=self.target[d],
            device_id_type=MESH,
        )

    def pack(self, own, info):
        face_send, face_recv, edge_send, edge_recv = self.refs
        for d, (dx, dy) in enumerate(DIRS):
            x = 7 if dx > 0 else 0
            y = 7 if dy > 0 else 0
            if d < 2:
                face_send[d, 0:8] = own[8 * x : 8 * x + 8]
            elif d < 4:
                for i in range(8):
                    face_send[d, i] = own[8 * i + y]
            else:
                edge_send[d - 4, 0] = own[8 * x + y]
            if d < 4:
                face_send[d, 8:11] = info
            else:
                edge_send[d - 4, 1:4] = info

    def start(self):
        _, face_recv, _, edge_recv = self.refs
        for d in range(8):
            @pl.when(self.there[d])
            def _():
                self.copy(d, OPPOSITE[d]).start()

            @pl.when(jnp.logical_not(self.there[d]))
            def _():
                recv = face_recv if d < 4 else edge_recv
                recv[d % 4] = jnp.zeros(recv.shape[1:], recv.dtype)

    def finish(self):
        for d in range(8):
            @pl.when(self.there[d])
            def _():
                copy = self.copy(d, d)
                copy.wait_send()
                copy.wait_recv()


def weights_of(place, meta, m, dx, dy):
    x, y, z = place
    base = [meta[m, i].astype(F32) for i in range(3)]
    same = (x == base[0] + float(dx)) & (y == base[1] + float(dy))
    step = z - base[2]
    here = jnp.where(same & (step == 0.0), 1.0, 0.0)
    below = jnp.where(same & (step == -1.0), 1.0, 0.0)
    above = jnp.where(same & (step == 1.0), 1.0, 0.0)
    level = iota(here.shape, 0)
    return jnp.where(level == 0, below, here), here, jnp.where(level == 7, above, here)


def shifted(block):
    width = block.shape[-1]
    flat = block.reshape(-1, 8, width)
    down = pltpu.roll(flat, 1, 1).reshape(block.shape)
    up = pltpu.roll(flat, 7, 1).reshape(block.shape)
    return down, block, up


def sum_sources(sources):
    total = None
    for block, weights in sources:
        terms = [part * weight for part, weight in zip(shifted(block), weights)]
        total = terms if total is None else [a + b for a, b in zip(total, terms)]
    return total


def put(window, at_x, at_y, per_slot):
    width = per_slot[0][0].shape[-1]
    for k in range(3):
        both = jnp.concatenate([parts[k] for parts in per_slot], 1).astype(BF)
        rows = both.shape[0]
        if at_x is None:
            for i in range(rows):
                window[i + 1, at_y, :, k * width : (k + 1) * width] = both[i]
        elif at_y is None:
            window[at_x, 1 : 1 + rows, :, k * width : (k + 1) * width] = both
        else:
            window[at_x, at_y, :, k * width : (k + 1) * width] = both[0]


def own_place(meta, s, width):
    return [jnp.full((8, width), meta[s, i].astype(F32), F32) for i in range(3)]


def build_centre(window, own, meta, slots):
    width = own.shape[-1]
    ones = jnp.ones((8, width), F32)
    level = iota((8, width), 0)
    self_weights = (jnp.where(level == 0, 0.0, ones), ones, jnp.where(level == 7, 0.0, ones))
    other = [
        [(s, weights_of(own_place(meta, s, width), meta, m, 0, 0)) for s in range(slots) if s != m]
        for m in range(slots)
    ]

    def step(x, carry):
        rows = own[pl.ds(8 * x, 8)].astype(F32)
        blocks = [rows[:, 8 * s : 8 * s + 8] for s in range(slots)]
        per_slot = []
        for m in range(slots):
            sources = [(blocks[m], self_weights)] + [(blocks[s], w) for s, w in other[m]]
            per_slot.append(sum_sources(sources))
        put(window, x + 1, None, per_slot)
        return carry

    lax.fori_loop(0, 8, step, 0)


def build_border(window, own, face_recv, edge_recv, meta, slots):
    width = own.shape[-1]
    for dx, dy in DIRS:
        x = {-1: 7, 0: None, 1: 0}[dx]
        y = {-1: 7, 0: None, 1: 0}[dy]
        if dx and dy:
            own_rows = own[8 * x + y][None]
        elif dx:
            own_rows = own[8 * x : 8 * x + 8]
        else:
            own_rows = jnp.stack([own[8 * i + y] for i in range(8)], 0)
        own_rows = own_rows.astype(F32)
        tiles = []
        if dx:
            ref, d = face_recv, DIRS.index((dx, 0))
            rows = ref[d, y : y + 1] if dy else ref[d, 0:8]
            tiles.append((rows, ref[d, 8:11], dx, 0))
        if dy:
            ref, d = face_recv, DIRS.index((0, dy))
            rows = ref[d, x : x + 1] if dx else ref[d, 0:8]
            tiles.append((rows, ref[d, 8:11], 0, dy))
        if dx and dy:
            d = DIRS.index((dx, dy)) - 4
            tiles.append((edge_recv[d, 0:1], edge_recv[d, 1:4], dx, dy))
        tiles = [(rows.astype(F32), info.astype(F32), tx, ty) for rows, info, tx, ty in tiles]
        per_slot = []
        for m in range(slots):
            sources = []
            for s in range(slots):
                span = slice(8 * s, 8 * s + 8)
                if s != m:
                    place = own_place(meta, s, width)
                    sources.append((own_rows[:, span], weights_of(place, meta, m, dx, dy)))
                for rows, info, tx, ty in tiles:
                    place = (
                        info[0, span] + float(FB_X * tx),
                        info[1, span] + float(FB_Y * ty),
                        info[2, span],
                    )
                    sources.append((rows[:, span], weights_of(place, meta, m, dx, dy)))
            per_slot.append(sum_sources(sources))
        put(
            window,
            None if not dx else (0 if dx < 0 else 9),
            None if not dy else (0 if dy < 0 else 9),
            per_slot,
        )


def patch(window, j):
    x, y = j // 3, j % 3
    view = window[pl.ds(x, 8), pl.ds(y, 8)]
    return view.reshape(64 * view.shape[2], view.shape[3])


class Ring:
    def __init__(self, index, count, target, send_sem, recv_sem):
        self.index, self.count = index, count
        self.sems = (send_sem, recv_sem)
        self.ranks = [lax.rem(index + r, count) for r in range(1, count)]
        self.origins = [lax.rem(index + count - r, count) for r in range(1, count)]
        self.targets = [target(rank) for rank in self.ranks]

    def copies(self, source, landing):
        return [
            pltpu.make_async_remote_copy(
                src_ref=source(i, self.ranks[i]),
                dst_ref=landing(i, self.index),
                send_sem=self.sems[0].at[i],
                recv_sem=self.sems[1].at[i],
                device_id=self.targets[i],
                device_id_type=MESH,
            )
            for i in range(self.count - 1)
        ]

    def start(self, source, landing):
        for copy in self.copies(source, landing):
            copy.start()

    def finish(self, source, arrived):
        sends = self.copies(source, arrived)
        for i, copy in enumerate(sends):
            copy.wait_send()
            pltpu.make_async_remote_copy(
                src_ref=source(i, self.ranks[i]),
                dst_ref=arrived(i, self.origins[i]),
                send_sem=self.sems[0].at[i],
                recv_sem=self.sems[1].at[i],
                device_id=self.targets[i],
                device_id_type=MESH,
            ).wait_recv()


def add_rows(target, own, arrived, count, rows, step):
    def body(i, carry):
        at = pl.multiple_of(i * step, step)
        total = own(at).astype(F32)
        for r in range(count):
            total = total + arrived[r, pl.ds(at, step)].astype(F32)
        target(at, total.astype(BF))
        return carry

    lax.fori_loop(0, rows // step, body, 0)


def store_to(ref, base):
    def store(at, value):
        ref[pl.ds(pl.multiple_of(base + at, 16), value.shape[0])] = value

    return store


def load_from(ref, base, step):
    return lambda at: ref[pl.ds(pl.multiple_of(base + at, 16), step)]


class Part:
    def __init__(self, order, chunk, base, sems, summed, partial, final, arrivals):
        (i, count, to_one), (j, others, to_two) = order
        self.i, self.j, self.chunk, self.base = i, j, chunk, base
        self.summed, self.partial, self.final = summed, partial, final
        self.arrivals = arrivals
        self.part = part = chunk * others
        self.mine = base + (i * others + j) * chunk
        self.rings = [
            Ring(i, count, to_one, *sems[0]),
            Ring(j, others, to_two, *sems[1]),
            Ring(j, others, to_two, *sems[2]),
            Ring(i, count, to_one, *sems[3]),
        ]
        wide = lambda r: pl.ds(pl.multiple_of(base + r * part, 16), part)
        thin = lambda r: pl.ds(pl.multiple_of(r * chunk, 16), chunk)
        cell = lambda r: pl.ds(pl.multiple_of(base + (i * others + r) * chunk, 16), chunk)
        self.source = [
            lambda n, r: summed.at[wide(r)],
            lambda n, r: partial.at[thin(r)],
            lambda n, r: final.at[cell(j)],
            lambda n, r: final.at[wide(i)],
        ]
        self.land = [
            lambda n, r: arrivals[0].at[n],
            lambda n, r: arrivals[1].at[n],
            lambda n, r: final.at[cell(r)],
            lambda n, r: final.at[wide(r)],
        ]

    def begin(self, n):
        self.rings[n].start(self.source[n], self.land[n])

    def end(self, n):
        self.rings[n].finish(self.source[n], self.land[n])

    def start_first(self):
        self.begin(0)

    def start_second(self):
        self.end(0)
        add_rows(
            store_to(self.partial, 0), load_from(self.summed, self.base + self.i * self.part, self.chunk),
            self.arrivals[0], self.rings[0].count - 1, self.part, self.chunk,
        )
        self.begin(1)

    def start_third(self):
        self.end(1)
        add_rows(
            store_to(self.final, self.mine), load_from(self.partial, self.j * self.chunk, 16),
            self.arrivals[1], self.rings[1].count - 1, self.chunk, 16,
        )
        self.begin(2)

    def start_fourth(self):
        self.end(2)
        self.begin(3)

    def finish(self):
        self.end(3)


class Plan:
    def __init__(self, sizes, channels):
        self.nx, self.ny = sizes
        self.inner = 4 if self.nx % 4 == 0 else 1
        self.outer = self.nx // self.inner
        self.rows = channels // self.ny
        self.padded = -(-self.rows // 16) * 16
        self.full = channels // 128
        self.tail = channels % 128
        self.per = 128 // self.tail if self.tail else 1
        self.groups = -(-27 // self.per) if self.tail else 0
        total = (27 * self.full + self.groups) * self.padded
        self.chunk = -(-total // (16 * self.nx)) * 16
        self.total = self.chunk * self.nx
        across = self.chunk // 48 * 16 if min(self.inner, self.outer) > 1 else 0
        self.chunks = [self.chunk - across] + ([across] if across else [])


def pack_weight_gradient(plan, stage, wide, width):
    rows, padded = plan.rows, plan.padded

    def piece(e, share, low, high):
        j, k = e // 3, e % 3
        value = wide[j, share * rows : (share + 1) * rows, k * width + low : k * width + high]
        if padded != rows:
            value = jnp.concatenate([value, jnp.zeros((padded - rows, high - low), F32)], 0)
        return value

    for share in range(plan.ny):
        at = 0
        for e in range(27):
            for tile in range(plan.full):
                block = piece(e, share, 128 * tile, 128 * tile + 128)
                stage[share, at : at + padded] = block.astype(BF)
                at += padded
        for g in range(plan.groups):
            parts = []
            for e in range(g * plan.per, (g + 1) * plan.per):
                low = 128 * plan.full
                parts.append(
                    piece(e, share, low, low + plan.tail)
                    if e < 27
                    else jnp.zeros((padded, plan.tail), F32)
                )
            stage[share, at : at + padded] = jnp.concatenate(parts, 1).astype(BF)
            at += padded
        if at < plan.total:
            stage[share, at:] = jnp.zeros((plan.total - at, 128), BF)


def unpack_weight_gradient(plan, final, out):
    rows, padded, tail = plan.rows, plan.padded, plan.tail
    at = 0
    for e in range(27):
        for tile in range(plan.full):
            out[e, :, 128 * tile : 128 * tile + 128] = final[at : at + padded].astype(F32)[:rows]
            at += padded
    for g in range(plan.groups):
        block = final[at : at + padded].astype(F32)[:rows]
        for i, e in enumerate(range(g * plan.per, min(27, (g + 1) * plan.per))):
            out[e, :, 128 * plan.full :] = block[:, i * tail : (i + 1) * tail]
        at += padded


def whole_kernel(
    sizes, plan, fine, coarse_place, parents, counts, skip, coarse, cot, up_raw, weight_raw,
    grad_skip, grad_coarse, grad_rows,
    own, window, acc, turned, up, weight, fetched, held, wide, stage, summed, partial, final,
    in_y, arrivals, fetch_sem,
    face_send, face_recv, edge_send, edge_recv, send_sem, recv_sem,
    face_send2, face_recv2, edge_send2, edge_recv2, send_sem2, recv_sem2,
    ring_send, ring_recv,
):
    slots, channels, voxels = skip.shape
    width = own.shape[-1]
    gx, gy = lax.axis_index("gx"), lax.axis_index("gy")
    first = Exchange(sizes, face_send, face_recv, edge_send, edge_recv, send_sem, recv_sem)
    second = Exchange(sizes, face_send2, face_recv2, edge_send2, edge_recv2, send_sem2, recv_sem2)
    inner, outer = plan.inner, plan.outer
    a, b = lax.rem(gx, inner), lax.div(gx, inner)

    def sems(i):
        return ring_send.at[i], ring_recv.at[i]

    ring_y = Ring(gy, plan.ny, lambda r: (gx, r), *sems(0))
    to_inner = lambda r: (b * inner + r, gy)
    to_outer = lambda r: (r * inner + a, gy)
    groups = ((a, inner, to_inner), (b, outer, to_outer))
    base, parts = 0, []
    for number, chunk in enumerate(plan.chunks):
        order = groups if number == 0 else groups[::-1]
        parts.append(
            Part(order, chunk, base, [sems(1 + 4 * number + i) for i in range(4)],
                 summed, partial[number], final, arrivals[2 * number : 2 * number + 2])
        )
        base += chunk * plan.nx
    others = ring_y.targets + parts[0].rings[0].targets + parts[0].rings[1].targets
    first.greet(others)
    fetches = [
        pltpu.make_async_copy(weight_raw, fetched, fetch_sem.at[0]),
        pltpu.make_async_copy(cot, held, fetch_sem.at[1]),
    ]
    for fetch in fetches:
        fetch.start()

    meta = {}
    for m in range(slots):
        parent = parents[m]
        for i in range(3):
            base = sum(
                jnp.where(parent == n, coarse_place[n, i], 0) for n in range(coarse.shape[0])
            )
            meta[m, i] = fine[m, i]
            meta[m, 3 + i] = fine[m, i] - 2 * base
        meta[m, 6] = parent
        meta[m, 7] = jnp.where(m < counts[0], 1, 0)
    info = jnp.stack(
        [
            jnp.concatenate(
                [jnp.full((8, width), meta[m, i].astype(F32), F32) for m in range(slots)], 0
            )
            for i in range(3)
        ],
        0,
    ).astype(BF)

    up[...] = jnp.zeros_like(up)
    for k in range(8):
        up[k * width : k * width + channels, 0:channels] = up_raw[k]
    eye = identity(voxels)
    spread = one_hot(iota((voxels, voxels), 1) == child_row(iota((voxels, 1), 0)))
    rows = []
    for m in range(slots):
        octant = None
        column = octant_column(iota((64, 1), 0), meta, m)
        for n in range(coarse.shape[0]):
            pick = one_hot(iota((64, voxels), 1) == jnp.where(meta[m, 6] == n, column, -1))
            part = dot(pick, padded_rows(coarse[n], width), NT)
            octant = part if octant is None else octant + part
        lifted = dot(octant.astype(BF), up[...], NT)
        lifted = jnp.concatenate([lifted[:, k * width : (k + 1) * width] for k in range(8)], 0)
        high = lifted.astype(BF)
        low = (lifted - high.astype(F32)).astype(BF)
        total = dot(spread, high) + dot(spread, low) + dot(eye, padded_rows(skip[m], width), NT)
        rows.append((total * meta[m, 7].astype(F32)).reshape(64, 8, width))
    own[...] = jnp.concatenate(rows, 1).astype(BF)
    first.pack(own, info)
    first.await_greetings(others)
    first.start()
    weight[...] = jnp.zeros_like(weight)
    fetches[0].wait()
    for e in range(27):
        low = (e % 3) * width
        weight[e // 3, 0:channels, low : low + channels] = fetched[e]
    build_centre(window, own, meta, slots)
    first.finish()
    build_border(window, own, face_recv, edge_recv, meta, slots)
    acc[...] = jnp.zeros_like(acc)

    def conv(j, carry):
        acc[...] += dot(patch(window, j), weight[j], NT)
        return carry

    lax.fori_loop(0, 9, conv, 0)
    pre_all = acc[...].reshape(64, 8 * slots, width)
    grads = []
    fetches[1].wait()
    for m in range(slots):
        pre = pre_all[:, 8 * m : 8 * m + 8].reshape(voxels, width)
        sigma = 1.0 / (1.0 + jnp.exp(-pre))
        value = dot(eye, padded_rows(held[m], width), NT)
        value = value * (sigma * (1.0 + pre * (1.0 - sigma))) * meta[m, 7].astype(F32)
        grads.append(value.reshape(64, 8, width))
    grad = jnp.concatenate(grads, 1)
    own[...] = grad.astype(BF)
    second.pack(own, info)
    second.start()
    turned[...] = jnp.transpose(grad.reshape(64 * 8 * slots, width)).astype(BF)

    def outer_product(j, carry):
        wide[j] = dot(turned[...], patch(window, j))
        return carry

    lax.fori_loop(0, 9, outer_product, 0)
    pack_weight_gradient(plan, stage, wide, width)

    source_y, land_y = (lambda i, r: stage.at[r]), (lambda i, r: in_y.at[i])
    ring_y.start(source_y, land_y)
    build_centre(window, own, meta, slots)
    ring_y.finish(source_y, land_y)
    add_rows(
        store_to(summed, 0), lambda at: stage[gy, pl.ds(at, plan.chunk)],
        in_y, plan.ny - 1, plan.total, plan.chunk,
    )
    for part in parts:
        part.start_first()

    second.finish()
    build_border(window, own, face_recv2, edge_recv2, meta, slots)
    acc[...] = jnp.zeros_like(acc)

    def conv_back(j, carry):
        rows = patch(window, j)
        value = None
        for k in range(3):
            term = dot(
                rows[:, k * width : (k + 1) * width],
                weight[8 - j, :, (2 - k) * width : (3 - k) * width],
            )
            value = term if value is None else value + term
        acc[...] += value
        return carry

    lax.fori_loop(0, 9, conv_back, 0)
    for part in parts:
        part.start_second()

    all_rows = acc[...].reshape(64, 8 * slots, width)
    gather = one_hot(iota((voxels, voxels), 0) == child_row(iota((1, voxels), 1)))
    folded = []
    for m in range(slots):
        rows = all_rows[:, 8 * m : 8 * m + 8].reshape(voxels, width) * meta[m, 7].astype(F32)
        grad_skip[m] = jnp.transpose(rows).astype(BF)[:channels]
        grouped = dot(gather, rows.astype(BF)).astype(BF)
        folded.append(jnp.concatenate([grouped[64 * k : 64 * k + 64] for k in range(8)], 1))

    for part in parts:
        part.start_third()
    folded = [jnp.transpose(dot(grouped, up[...])).astype(BF) for grouped in folded]
    for part in parts:
        part.start_fourth()
    for n in range(grad_coarse.shape[0]):
        value = None
        for m in range(slots):
            column = octant_column(iota((64, 1), 0), meta, m)
            place = one_hot(iota((64, voxels), 1) == jnp.where(meta[m, 6] == n, column, -1))
            term = dot(folded[m], place)
            value = term if value is None else value + term
        grad_coarse[n] = value.astype(BF)[:channels]
    for part in parts:
        part.finish()
    grad_rows[...] = final[...]


def output_kernel(plan, skip_in, coarse_in, rows_in, skip_out, coarse_out, conv_out):
    skip_out[...] = skip_in[...]
    coarse_out[...] = coarse_in[...]
    unpack_weight_gradient(plan, rows_in, conv_out)


def exchange_scratch(slots, width):
    return [
        pltpu.VMEM((4, 11, 8 * slots, width), BF),
        pltpu.VMEM((4, 11, 8 * slots, width), BF),
        pltpu.VMEM((4, 4, 8 * slots, width), BF),
        pltpu.VMEM((4, 4, 8 * slots, width), BF),
        pltpu.SemaphoreType.DMA((8,)),
        pltpu.SemaphoreType.DMA((8,)),
    ]


def local(
    sizes, skip_feature_rows, coarse_features, cotangent, fine_coords, coarse_coords,
    parents, counts, conv_weight, up_weight,
):
    slots, channels, voxels = skip_feature_rows.shape
    width = -(-channels // 128) * 128
    plan = Plan(sizes, channels)
    peers = max(plan.ny, plan.inner, plan.outer, 2) - 1
    smem = pl.BlockSpec(memory_space=pltpu.SMEM)
    vmem = pl.BlockSpec(memory_space=pltpu.VMEM)
    anywhere = pl.BlockSpec(memory_space=pl.ANY)
    cells = 64 * 8 * slots
    partials, arrivals = [], []
    for number, chunk in enumerate(plan.chunks):
        sides = (plan.inner, plan.outer) if number == 0 else (plan.outer, plan.inner)
        partials.append(pltpu.VMEM((chunk * sides[1], 128), BF))
        arrivals.append(pltpu.VMEM((max(sides[0] - 1, 1), chunk * sides[1], 128), BF))
        arrivals.append(pltpu.VMEM((max(sides[1] - 1, 1), chunk, 128), BF))
    grad_skip, grad_coarse, grad_rows = pl.pallas_call(
        functools.partial(whole_kernel, sizes, plan),
        out_shape=(
            jax.ShapeDtypeStruct((slots, channels, voxels), BF),
            jax.ShapeDtypeStruct(coarse_features.shape, BF),
            jax.ShapeDtypeStruct((plan.total, 128), BF),
        ),
        in_specs=[smem] * 4 + [vmem, vmem, anywhere, vmem, anywhere],
        out_specs=(vmem, vmem, vmem),
        scratch_shapes=[
            pltpu.VMEM((64, 8 * slots, width), BF),
            pltpu.VMEM((10, 10, 8 * slots, 3 * width), BF),
            pltpu.VMEM((cells, width), F32),
            pltpu.VMEM((width, cells), BF),
            pltpu.VMEM((8 * width, width), BF),
            pltpu.VMEM((9, width, 3 * width), BF),
            pltpu.VMEM((27, channels, channels), BF),
            pltpu.VMEM((slots, channels, voxels), BF),
            pltpu.VMEM((9, width, 3 * width), F32),
            pltpu.VMEM((plan.ny, plan.total, 128), BF),
            pltpu.VMEM((plan.total, 128), BF),
            tuple(partials),
            pltpu.VMEM((plan.total, 128), BF),
            pltpu.VMEM((max(plan.ny - 1, 1), plan.total, 128), BF),
            tuple(arrivals),
            pltpu.SemaphoreType.DMA((2,)),
        ]
        + exchange_scratch(slots, width)
        + exchange_scratch(slots, width)
        + [pltpu.SemaphoreType.DMA((9, peers)), pltpu.SemaphoreType.DMA((9, peers))],
        compiler_params=pltpu.CompilerParams(
            collective_id=0, has_side_effects=True, vmem_limit_bytes=60 * 1024 * 1024
        ),
        cost_estimate=pl.CostEstimate(
            flops=6 * 27 * slots * voxels * channels * channels,
            bytes_accessed=12 << 20, transcendentals=0,
        ),
        name="whole",
    )(
        fine_coords, coarse_coords, parents, counts,
        skip_feature_rows, coarse_features, cotangent, up_weight,
        conv_weight.transpose(1, 0, 2),
    )
    grad_skip, grad_coarse, grad_conv = pl.pallas_call(
        functools.partial(output_kernel, plan),
        out_shape=(
            jax.ShapeDtypeStruct(grad_skip.shape, BF),
            jax.ShapeDtypeStruct(grad_coarse.shape, BF),
            jax.ShapeDtypeStruct((27, plan.rows, channels), F32),
        ),
        in_specs=[vmem] * 3,
        out_specs=(vmem, vmem, vmem),
        compiler_params=pltpu.CompilerParams(vmem_limit_bytes=60 * 1024 * 1024),
        name="outputs",
    )(grad_skip, grad_coarse, grad_rows)
    return (grad_skip, grad_coarse, grad_conv.transpose(1, 0, 2))


def solution(mesh):
    in_specs = (
        P(("gx", "gy"), None, None),
        P(("gx", "gy"), None, None),
        P(("gx", "gy"), None, None),
        P(("gx", "gy"), None),
        P(("gx", "gy"), None),
        P(("gx", "gy")),
        P(("gx", "gy")),
        P(),
        P(),
    )
    out_specs = (P(("gx", "gy"), None, None), P(("gx", "gy"), None, None), P("gy", None, None))
    sizes = (mesh.shape["gx"], mesh.shape["gy"])
    return jax.shard_map(
        functools.partial(local, sizes),
        mesh=mesh,
        in_specs=in_specs,
        out_specs=out_specs,
        check_vma=False,
    )
```

```python
import functools

import jax
import jax.numpy as jnp
from jax import lax
from jax.experimental import pallas as pl
from jax.experimental.pallas import tpu as pltpu
from jax.sharding import PartitionSpec as P

FB_X = 2
FB_Y = 2
MESH = pl.DeviceIdType.MESH
BF = jnp.bfloat16
F32 = jnp.float32
DIRS = ((-1, 0), (1, 0), (0, -1), (0, 1), (-1, -1), (-1, 1), (1, -1), (1, 1))
OPPOSITE = tuple(DIRS.index((-dx, -dy)) for dx, dy in DIRS)
NT = (((1,), (1,)), ((), ()))


def dot(a, b, dims=(((1,), (0,)), ((), ()))):
    return lax.dot_general(a, b, dims, preferred_element_type=F32)


def iota(shape, dim):
    return lax.broadcasted_iota(jnp.int32, shape, dim)


def one_hot(cond):
    return jnp.where(cond, 1.0, 0.0).astype(BF)


def identity(n):
    return one_hot(iota((n, n), 0) == iota((n, n), 1))


def child_row(v):
    p, q, s = v >> 6, (v >> 3) & 7, v & 7
    k = 4 * (p & 1) + 2 * (q & 1) + (s & 1)
    return k * 64 + (p >> 1) * 16 + (q >> 1) * 4 + (s >> 1)


def octant_column(u, meta, m):
    return (
        64 * (4 * meta[m, 3] + (u >> 4))
        + 8 * (4 * meta[m, 4] + ((u >> 2) & 3))
        + 4 * meta[m, 5]
        + (u & 3)
    )


def padded_rows(block, width):
    extra = width - block.shape[0]
    if extra == 0:
        return block
    return jnp.concatenate([block, jnp.zeros((extra, block.shape[1]), block.dtype)], 0)


class Exchange:
    def __init__(self, sizes, face_send, face_recv, edge_send, edge_recv, send_sem, recv_sem):
        gx, gy = lax.axis_index("gx"), lax.axis_index("gy")
        nx, ny = sizes
        self.refs = (face_send, face_recv, edge_send, edge_recv)
        self.sems = (send_sem, recv_sem)
        self.there, self.target = [], []
        for dx, dy in DIRS:
            x, y = gx + dx, gy + dy
            self.there.append((x >= 0) & (x < nx) & (y >= 0) & (y < ny))
            self.target.append((x, y))

    def greet(self, others):
        barrier = pltpu.get_barrier_semaphore()
        for d in range(8):
            @pl.when(self.there[d])
            def _():
                pl.semaphore_signal(barrier, inc=1, device_id=self.target[d], device_id_type=MESH)

        for target in others:
            pl.semaphore_signal(barrier, inc=1, device_id=target, device_id_type=MESH)

    def await_greetings(self, others):
        peers = len(others) + sum(there.astype(jnp.int32) for there in self.there)
        pl.semaphore_wait(pltpu.get_barrier_semaphore(), peers)

    def copy(self, d, landing):
        face_send, face_recv, edge_send, edge_recv = self.refs
        send, recv = (face_send, face_recv) if d < 4 else (edge_send, edge_recv)
        return pltpu.make_async_remote_copy(
            src_ref=send.at[d % 4],
            dst_ref=recv.at[landing % 4],
            send_sem=self.sems[0].at[d],
            recv_sem=self.sems[1].at[landing],
            device_id=self.target[d],
            device_id_type=MESH,
        )

    def pack(self, own, info):
        face_send, face_recv, edge_send, edge_recv = self.refs
        for d, (dx, dy) in enumerate(DIRS):
            x = 7 if dx > 0 else 0
            y = 7 if dy > 0 else 0
            if d < 2:
                face_send[d, 0:8] = own[8 * x : 8 * x + 8]
            elif d < 4:
                for i in range(8):
                    face_send[d, i] = own[8 * i + y]
            else:
                edge_send[d - 4, 0] = own[8 * x + y]
            if d < 4:
                face_send[d, 8:11] = info
            else:
                edge_send[d - 4, 1:4] = info

    def start(self):
        _, face_recv, _, edge_recv = self.refs
        for d in range(8):
            @pl.when(self.there[d])
            def _():
                self.copy(d, OPPOSITE[d]).start()

            @pl.when(jnp.logical_not(self.there[d]))
            def _():
                recv = face_recv if d < 4 else edge_recv
                recv[d % 4] = jnp.zeros(recv.shape[1:], recv.dtype)

    def finish(self):
        for d in range(8):
            @pl.when(self.there[d])
            def _():
                copy = self.copy(d, d)
                copy.wait_send()
                copy.wait_recv()


def weights_of(place, meta, m, dx, dy):
    x, y, z = place
    base = [meta[m, i].astype(F32) for i in range(3)]
    same = (x == base[0] + float(dx)) & (y == base[1] + float(dy))
    step = z - base[2]
    here = jnp.where(same & (step == 0.0), 1.0, 0.0)
    below = jnp.where(same & (step == -1.0), 1.0, 0.0)
    above = jnp.where(same & (step == 1.0), 1.0, 0.0)
    level = iota(here.shape, 0)
    return jnp.where(level == 7, below, here), here, jnp.where(level == 0, above, here)


def rolled(block, step):
    flat = block.reshape(-1, 8, block.shape[-1])
    return pltpu.roll(flat, step, 1).reshape(block.shape)


def sum_sources(sources):
    total = None
    for block, weights in sources:
        terms = [block if weight is None else block * weight for weight in weights]
        total = terms if total is None else [a + b for a, b in zip(total, terms)]
    return rolled(total[0], 1), total[1], rolled(total[2], 7)


def put(window, at_x, at_y, per_slot):
    width = per_slot[0][0].shape[-1]
    for k in range(3):
        both = jnp.concatenate([parts[k] for parts in per_slot], 1).astype(BF)
        rows = both.shape[0]
        if at_x is None:
            for i in range(rows):
                window[i + 1, at_y, :, k * width : (k + 1) * width] = both[i]
        elif at_y is None:
            window[at_x, 1 : 1 + rows, :, k * width : (k + 1) * width] = both
        else:
            window[at_x, at_y, :, k * width : (k + 1) * width] = both[0]


def own_place(meta, s, width):
    return [jnp.full((8, width), meta[s, i].astype(F32), F32) for i in range(3)]


def build_centre(window, own, meta, slots):
    width = own.shape[-1]
    ones = jnp.ones((8, width), F32)
    level = iota((8, width), 0)
    self_weights = (jnp.where(level == 7, 0.0, ones), None, jnp.where(level == 0, 0.0, ones))
    other = [
        [(s, weights_of(own_place(meta, s, width), meta, m, 0, 0)) for s in range(slots) if s != m]
        for m in range(slots)
    ]

    def step(x, carry):
        rows = own[pl.ds(8 * x, 8)].astype(F32)
        blocks = [rows[:, 8 * s : 8 * s + 8] for s in range(slots)]
        per_slot = []
        for m in range(slots):
            sources = [(blocks[m], self_weights)] + [(blocks[s], w) for s, w in other[m]]
            per_slot.append(sum_sources(sources))
        put(window, x + 1, None, per_slot)
        return carry

    lax.fori_loop(0, 8, step, 0)


def build_border(window, own, face_recv, edge_recv, meta, slots):
    width = own.shape[-1]
    for dx, dy in DIRS:
        x = {-1: 7, 0: None, 1: 0}[dx]
        y = {-1: 7, 0: None, 1: 0}[dy]
        if dx and dy:
            own_rows = own[8 * x + y][None]
        elif dx:
            own_rows = own[8 * x : 8 * x + 8]
        else:
            own_rows = jnp.stack([own[8 * i + y] for i in range(8)], 0)
        own_rows = own_rows.astype(F32)
        tiles = []
        if dx:
            ref, d = face_recv, DIRS.index((dx, 0))
            rows = ref[d, y : y + 1] if dy else ref[d, 0:8]
            tiles.append((rows, ref[d, 8:11], dx, 0))
        if dy:
            ref, d = face_recv, DIRS.index((0, dy))
            rows = ref[d, x : x + 1] if dx else ref[d, 0:8]
            tiles.append((rows, ref[d, 8:11], 0, dy))
        if dx and dy:
            d = DIRS.index((dx, dy)) - 4
            tiles.append((edge_recv[d, 0:1], edge_recv[d, 1:4], dx, dy))
        tiles = [(rows.astype(F32), info.astype(F32), tx, ty) for rows, info, tx, ty in tiles]
        per_slot = []
        for m in range(slots):
            sources = []
            for s in range(slots):
                span = slice(8 * s, 8 * s + 8)
                if s != m:
                    place = own_place(meta, s, width)
                    sources.append((own_rows[:, span], weights_of(place, meta, m, dx, dy)))
                for rows, info, tx, ty in tiles:
                    place = (
                        info[0, span] + float(FB_X * tx),
                        info[1, span] + float(FB_Y * ty),
                        info[2, span],
                    )
                    sources.append((rows[:, span], weights_of(place, meta, m, dx, dy)))
            per_slot.append(sum_sources(sources))
        put(
            window,
            None if not dx else (0 if dx < 0 else 9),
            None if not dy else (0 if dy < 0 else 9),
            per_slot,
        )


def patch(window, j):
    x, y = j // 3, j % 3
    view = window[pl.ds(x, 8), pl.ds(y, 8)]
    return view.reshape(64 * view.shape[2], view.shape[3])


class Ring:
    def __init__(self, index, count, target, send_sem, recv_sem):
        self.index, self.count = index, count
        self.sems = (send_sem, recv_sem)
        self.ranks = [lax.rem(index + r, count) for r in range(1, count)]
        self.origins = [lax.rem(index + count - r, count) for r in range(1, count)]
        self.targets = [target(rank) for rank in self.ranks]

    def copies(self, source, landing):
        return [
            pltpu.make_async_remote_copy(
                src_ref=source(i, self.ranks[i]),
                dst_ref=landing(i, self.index),
                send_sem=self.sems[0].at[i],
                recv_sem=self.sems[1].at[i],
                device_id=self.targets[i],
                device_id_type=MESH,
            )
            for i in range(self.count - 1)
        ]

    def start(self, source, landing):
        for copy in self.copies(source, landing):
            copy.start()

    def finish(self, source, arrived):
        sends = self.copies(source, arrived)
        for i, copy in enumerate(sends):
            copy.wait_send()
            pltpu.make_async_remote_copy(
                src_ref=source(i, self.ranks[i]),
                dst_ref=arrived(i, self.origins[i]),
                send_sem=self.sems[0].at[i],
                recv_sem=self.sems[1].at[i],
                device_id=self.targets[i],
                device_id_type=MESH,
            ).wait_recv()


def add_rows(target, own, arrived, count, rows, step):
    def body(i, carry):
        at = pl.multiple_of(i * step, step)
        total = own(at).astype(F32)
        for r in range(count):
            total = total + arrived[r, pl.ds(at, step)].astype(F32)
        target(at, total.astype(BF))
        return carry

    lax.fori_loop(0, rows // step, body, 0)


def store_to(ref, base):
    def store(at, value):
        ref[pl.ds(pl.multiple_of(base + at, 16), value.shape[0])] = value

    return store


def load_from(ref, base, step):
    return lambda at: ref[pl.ds(pl.multiple_of(base + at, 16), step)]


class Part:
    def __init__(self, order, chunk, base, sems, summed, partial, final, arrivals):
        (i, count, to_one), (j, others, to_two) = order
        self.i, self.j, self.chunk, self.base = i, j, chunk, base
        self.summed, self.partial, self.final = summed, partial, final
        self.arrivals = arrivals
        self.part = part = chunk * others
        self.mine = base + (i * others + j) * chunk
        self.rings = [
            Ring(i, count, to_one, *sems[0]),
            Ring(j, others, to_two, *sems[1]),
            Ring(j, others, to_two, *sems[2]),
            Ring(i, count, to_one, *sems[3]),
        ]
        wide = lambda r: pl.ds(pl.multiple_of(base + r * part, 16), part)
        thin = lambda r: pl.ds(pl.multiple_of(r * chunk, 16), chunk)
        cell = lambda r: pl.ds(pl.multiple_of(base + (i * others + r) * chunk, 16), chunk)
        self.source = [
            lambda n, r: summed.at[wide(r)],
            lambda n, r: partial.at[thin(r)],
            lambda n, r: final.at[cell(j)],
            lambda n, r: final.at[wide(i)],
        ]
        self.land = [
            lambda n, r: arrivals[0].at[n],
            lambda n, r: arrivals[1].at[n],
            lambda n, r: final.at[cell(r)],
            lambda n, r: final.at[wide(r)],
        ]

    def begin(self, n):
        self.rings[n].start(self.source[n], self.land[n])

    def end(self, n):
        self.rings[n].finish(self.source[n], self.land[n])

    def start_first(self):
        self.begin(0)

    def start_second(self):
        self.end(0)
        add_rows(
            store_to(self.partial, 0), load_from(self.summed, self.base + self.i * self.part, self.chunk),
            self.arrivals[0], self.rings[0].count - 1, self.part, self.chunk,
        )
        self.begin(1)

    def start_third(self):
        self.end(1)
        add_rows(
            store_to(self.final, self.mine), load_from(self.partial, self.j * self.chunk, 16),
            self.arrivals[1], self.rings[1].count - 1, self.chunk, 16,
        )
        self.begin(2)

    def start_fourth(self):
        self.end(2)
        self.begin(3)

    def finish(self):
        self.end(3)


class Plan:
    def __init__(self, sizes, channels):
        self.nx, self.ny = sizes
        self.inner = 4 if self.nx % 4 == 0 else 1
        self.outer = self.nx // self.inner
        self.rows = channels // self.ny
        self.padded = -(-self.rows // 16) * 16
        self.full = channels // 128
        self.tail = channels % 128
        self.per = 128 // self.tail if self.tail else 1
        self.groups = -(-27 // self.per) if self.tail else 0
        total = (27 * self.full + self.groups) * self.padded
        self.chunk = -(-total // (16 * self.nx)) * 16
        self.total = self.chunk * self.nx
        across = self.chunk // 48 * 16 if min(self.inner, self.outer) > 1 else 0
        self.chunks = [self.chunk - across] + ([across] if across else [])


def pack_weight_gradient(plan, stage, wide, width):
    rows, padded = plan.rows, plan.padded

    def piece(e, share, low, high):
        j, k = e // 3, e % 3
        value = wide[j, share * rows : (share + 1) * rows, k * width + low : k * width + high]
        if padded != rows:
            value = jnp.concatenate([value, jnp.zeros((padded - rows, high - low), F32)], 0)
        return value

    for share in range(plan.ny):
        at = 0
        for e in range(27):
            for tile in range(plan.full):
                block = piece(e, share, 128 * tile, 128 * tile + 128)
                stage[share, at : at + padded] = block.astype(BF)
                at += padded
        for g in range(plan.groups):
            parts = []
            for e in range(g * plan.per, (g + 1) * plan.per):
                low = 128 * plan.full
                parts.append(
                    piece(e, share, low, low + plan.tail)
                    if e < 27
                    else jnp.zeros((padded, plan.tail), F32)
                )
            stage[share, at : at + padded] = jnp.concatenate(parts, 1).astype(BF)
            at += padded
        if at < plan.total:
            stage[share, at:] = jnp.zeros((plan.total - at, 128), BF)


def unpack_weight_gradient(plan, final, out):
    rows, padded, tail = plan.rows, plan.padded, plan.tail
    at = 0
    for e in range(27):
        for tile in range(plan.full):
            out[e, :, 128 * tile : 128 * tile + 128] = final[at : at + padded].astype(F32)[:rows]
            at += padded
    for g in range(plan.groups):
        block = final[at : at + padded].astype(F32)[:rows]
        for i, e in enumerate(range(g * plan.per, min(27, (g + 1) * plan.per))):
            out[e, :, 128 * plan.full :] = block[:, i * tail : (i + 1) * tail]
        at += padded


def whole_kernel(
    sizes, plan, fine, coarse_place, parents, counts, skip, coarse, cot, up_raw, weight_raw,
    grad_skip, grad_coarse, grad_rows,
    own, window, acc, turned, up, weight, fetched, held, wide, stage, summed, partial, final,
    in_y, arrivals, fetch_sem,
    face_send, face_recv, edge_send, edge_recv, send_sem, recv_sem,
    face_send2, face_recv2, edge_send2, edge_recv2, send_sem2, recv_sem2,
    ring_send, ring_recv,
):
    slots, channels, voxels = skip.shape
    width = own.shape[-1]
    gx, gy = lax.axis_index("gx"), lax.axis_index("gy")
    first = Exchange(sizes, face_send, face_recv, edge_send, edge_recv, send_sem, recv_sem)
    second = Exchange(sizes, face_send2, face_recv2, edge_send2, edge_recv2, send_sem2, recv_sem2)
    inner, outer = plan.inner, plan.outer
    a, b = lax.rem(gx, inner), lax.div(gx, inner)

    def sems(i):
        return ring_send.at[i], ring_recv.at[i]

    ring_y = Ring(gy, plan.ny, lambda r: (gx, r), *sems(0))
    to_inner = lambda r: (b * inner + r, gy)
    to_outer = lambda r: (r * inner + a, gy)
    groups = ((a, inner, to_inner), (b, outer, to_outer))
    base, parts = 0, []
    for number, chunk in enumerate(plan.chunks):
        order = groups if number == 0 else groups[::-1]
        parts.append(
            Part(order, chunk, base, [sems(1 + 4 * number + i) for i in range(4)],
                 summed, partial[number], final, arrivals[2 * number : 2 * number + 2])
        )
        base += chunk * plan.nx
    others = ring_y.targets + parts[0].rings[0].targets + parts[0].rings[1].targets
    first.greet(others)
    fetches = [
        pltpu.make_async_copy(weight_raw, fetched, fetch_sem.at[0]),
        pltpu.make_async_copy(cot, held, fetch_sem.at[1]),
    ]
    for fetch in fetches:
        fetch.start()

    meta = {}
    for m in range(slots):
        parent = parents[m]
        for i in range(3):
            base = sum(
                jnp.where(parent == n, coarse_place[n, i], 0) for n in range(coarse.shape[0])
            )
            meta[m, i] = fine[m, i]
            meta[m, 3 + i] = fine[m, i] - 2 * base
        meta[m, 6] = parent
        meta[m, 7] = jnp.where(m < counts[0], 1, 0)
    info = jnp.stack(
        [
            jnp.concatenate(
                [jnp.full((8, width), meta[m, i].astype(F32), F32) for m in range(slots)], 0
            )
            for i in range(3)
        ],
        0,
    ).astype(BF)

    up[...] = jnp.zeros_like(up)
    for k in range(8):
        up[k * width : k * width + channels, 0:channels] = up_raw[k]
    eye = identity(voxels)
    spread = one_hot(iota((voxels, voxels), 1) == child_row(iota((voxels, 1), 0)))
    rows = []
    for m in range(slots):
        octant = None
        column = octant_column(iota((64, 1), 0), meta, m)
        for n in range(coarse.shape[0]):
            pick = one_hot(iota((64, voxels), 1) == jnp.where(meta[m, 6] == n, column, -1))
            part = dot(pick, padded_rows(coarse[n], width), NT)
            octant = part if octant is None else octant + part
        lifted = dot(octant.astype(BF), up[...], NT)
        lifted = jnp.concatenate([lifted[:, k * width : (k + 1) * width] for k in range(8)], 0)
        high = lifted.astype(BF)
        low = (lifted - high.astype(F32)).astype(BF)
        total = dot(spread, high) + dot(spread, low) + dot(eye, padded_rows(skip[m], width), NT)
        rows.append((total * meta[m, 7].astype(F32)).reshape(64, 8, width))
    own[...] = jnp.concatenate(rows, 1).astype(BF)
    first.pack(own, info)
    first.await_greetings(others)
    first.start()
    weight[...] = jnp.zeros_like(weight)
    fetches[0].wait()
    for e in range(27):
        low = (e % 3) * width
        weight[e // 3, 0:channels, low : low + channels] = fetched[e]
    build_centre(window, own, meta, slots)
    first.finish()
    build_border(window, own, face_recv, edge_recv, meta, slots)
    acc[...] = jnp.zeros_like(acc)

    def conv(j, carry):
        acc[...] += dot(patch(window, j), weight[j], NT)
        return carry

    lax.fori_loop(0, 9, conv, 0)
    pre_all = acc[...].reshape(64, 8 * slots, width)
    grads = []
    fetches[1].wait()
    for m in range(slots):
        pre = pre_all[:, 8 * m : 8 * m + 8].reshape(voxels, width)
        sigma = 1.0 / (1.0 + jnp.exp(-pre))
        value = dot(eye, padded_rows(held[m], width), NT)
        value = value * (sigma * (1.0 + pre * (1.0 - sigma))) * meta[m, 7].astype(F32)
        grads.append(value.reshape(64, 8, width))
    grad = jnp.concatenate(grads, 1)
    own[...] = grad.astype(BF)
    second.pack(own, info)
    second.start()
    turned[...] = jnp.transpose(grad.reshape(64 * 8 * slots, width)).astype(BF)

    def outer_product(j, carry):
        wide[j] = dot(turned[...], patch(window, j))
        return carry

    lax.fori_loop(0, 9, outer_product, 0)
    pack_weight_gradient(plan, stage, wide, width)

    source_y, land_y = (lambda i, r: stage.at[r]), (lambda i, r: in_y.at[i])
    ring_y.start(source_y, land_y)
    build_centre(window, own, meta, slots)
    ring_y.finish(source_y, land_y)
    add_rows(
        store_to(summed, 0), lambda at: stage[gy, pl.ds(at, plan.chunk)],
        in_y, plan.ny - 1, plan.total, plan.chunk,
    )
    for part in parts:
        part.start_first()

    second.finish()
    build_border(window, own, face_recv2, edge_recv2, meta, slots)
    acc[...] = jnp.zeros_like(acc)

    def conv_back(j, carry):
        rows = patch(window, j)
        value = None
        for k in range(3):
            term = dot(
                rows[:, k * width : (k + 1) * width],
                weight[8 - j, :, (2 - k) * width : (3 - k) * width],
            )
            value = term if value is None else value + term
        acc[...] += value
        return carry

    lax.fori_loop(0, 4, conv_back, 0)
    for part in parts:
        part.start_second()
    lax.fori_loop(4, 9, conv_back, 0)
    for part in parts:
        part.start_third()

    all_rows = acc[...].reshape(64, 8 * slots, width)
    gather = one_hot(iota((voxels, voxels), 0) == child_row(iota((1, voxels), 1)))
    folded = []
    for m in range(slots):
        rows = all_rows[:, 8 * m : 8 * m + 8].reshape(voxels, width) * meta[m, 7].astype(F32)
        grad_skip[m] = jnp.transpose(rows).astype(BF)[:channels]
        grouped = dot(gather, rows.astype(BF)).astype(BF)
        folded.append(jnp.concatenate([grouped[64 * k : 64 * k + 64] for k in range(8)], 1))

    for part in parts:
        part.start_fourth()
    folded = [jnp.transpose(dot(grouped, up[...])).astype(BF) for grouped in folded]
    for n in range(grad_coarse.shape[0]):
        value = None
        for m in range(slots):
            column = octant_column(iota((64, 1), 0), meta, m)
            place = one_hot(iota((64, voxels), 1) == jnp.where(meta[m, 6] == n, column, -1))
            term = dot(folded[m], place)
            value = term if value is None else value + term
        grad_coarse[n] = value.astype(BF)[:channels]
    for part in parts:
        part.finish()
    grad_rows[...] = final[...]


def output_kernel(plan, skip_in, coarse_in, rows_in, skip_out, coarse_out, conv_out):
    skip_out[...] = skip_in[...]
    coarse_out[...] = coarse_in[...]
    unpack_weight_gradient(plan, rows_in, conv_out)


def exchange_scratch(slots, width):
    return [
        pltpu.VMEM((4, 11, 8 * slots, width), BF),
        pltpu.VMEM((4, 11, 8 * slots, width), BF),
        pltpu.VMEM((4, 4, 8 * slots, width), BF),
        pltpu.VMEM((4, 4, 8 * slots, width), BF),
        pltpu.SemaphoreType.DMA((8,)),
        pltpu.SemaphoreType.DMA((8,)),
    ]


def local(
    sizes, skip_feature_rows, coarse_features, cotangent, fine_coords, coarse_coords,
    parents, counts, conv_weight, up_weight,
):
    slots, channels, voxels = skip_feature_rows.shape
    width = -(-channels // 128) * 128
    plan = Plan(sizes, channels)
    peers = max(plan.ny, plan.inner, plan.outer, 2) - 1
    smem = pl.BlockSpec(memory_space=pltpu.SMEM)
    vmem = pl.BlockSpec(memory_space=pltpu.VMEM)
    anywhere = pl.BlockSpec(memory_space=pl.ANY)
    cells = 64 * 8 * slots
    partials, arrivals = [], []
    for number, chunk in enumerate(plan.chunks):
        sides = (plan.inner, plan.outer) if number == 0 else (plan.outer, plan.inner)
        partials.append(pltpu.VMEM((chunk * sides[1], 128), BF))
        arrivals.append(pltpu.VMEM((max(sides[0] - 1, 1), chunk * sides[1], 128), BF))
        arrivals.append(pltpu.VMEM((max(sides[1] - 1, 1), chunk, 128), BF))
    grad_skip, grad_coarse, grad_rows = pl.pallas_call(
        functools.partial(whole_kernel, sizes, plan),
        out_shape=(
            jax.ShapeDtypeStruct((slots, channels, voxels), BF),
            jax.ShapeDtypeStruct(coarse_features.shape, BF),
            jax.ShapeDtypeStruct((plan.total, 128), BF),
        ),
        in_specs=[smem] * 4 + [vmem, vmem, anywhere, vmem, anywhere],
        out_specs=(vmem, vmem, vmem),
        scratch_shapes=[
            pltpu.VMEM((64, 8 * slots, width), BF),
            pltpu.VMEM((10, 10, 8 * slots, 3 * width), BF),
            pltpu.VMEM((cells, width), F32),
            pltpu.VMEM((width, cells), BF),
            pltpu.VMEM((8 * width, width), BF),
            pltpu.VMEM((9, width, 3 * width), BF),
            pltpu.VMEM((27, channels, channels), BF),
            pltpu.VMEM((slots, channels, voxels), BF),
            pltpu.VMEM((9, width, 3 * width), F32),
            pltpu.VMEM((plan.ny, plan.total, 128), BF),
            pltpu.VMEM((plan.total, 128), BF),
            tuple(partials),
            pltpu.VMEM((plan.total, 128), BF),
            pltpu.VMEM((max(plan.ny - 1, 1), plan.total, 128), BF),
            tuple(arrivals),
            pltpu.SemaphoreType.DMA((2,)),
        ]
        + exchange_scratch(slots, width)
        + exchange_scratch(slots, width)
        + [pltpu.SemaphoreType.DMA((9, peers)), pltpu.SemaphoreType.DMA((9, peers))],
        compiler_params=pltpu.CompilerParams(
            collective_id=0, has_side_effects=True, vmem_limit_bytes=60 * 1024 * 1024
        ),
        cost_estimate=pl.CostEstimate(
            flops=6 * 27 * slots * voxels * channels * channels,
            bytes_accessed=12 << 20, transcendentals=0,
        ),
        name="whole",
    )(
        fine_coords, coarse_coords, parents, counts,
        skip_feature_rows, coarse_features, cotangent, up_weight,
        conv_weight.transpose(1, 0, 2),
    )
    grad_skip, grad_coarse, grad_conv = pl.pallas_call(
        functools.partial(output_kernel, plan),
        out_shape=(
            jax.ShapeDtypeStruct(grad_skip.shape, BF),
            jax.ShapeDtypeStruct(grad_coarse.shape, BF),
            jax.ShapeDtypeStruct((27, plan.rows, channels), F32),
        ),
        in_specs=[vmem] * 3,
        out_specs=(vmem, vmem, vmem),
        compiler_params=pltpu.CompilerParams(vmem_limit_bytes=60 * 1024 * 1024),
        name="outputs",
    )(grad_skip, grad_coarse, grad_rows)
    return (grad_skip, grad_coarse, grad_conv.transpose(1, 0, 2))


def solution(mesh):
    in_specs = (
        P(("gx", "gy"), None, None),
        P(("gx", "gy"), None, None),
        P(("gx", "gy"), None, None),
        P(("gx", "gy"), None),
        P(("gx", "gy"), None),
        P(("gx", "gy")),
        P(("gx", "gy")),
        P(),
        P(),
    )
    out_specs = (P(("gx", "gy"), None, None), P(("gx", "gy"), None, None), P("gy", None, None))
    sizes = (mesh.shape["gx"], mesh.shape["gy"])
    return jax.shard_map(
        functools.partial(local, sizes),
        mesh=mesh,
        in_specs=in_specs,
        out_specs=out_specs,
        check_vma=False,
    )
```

```python
import functools

import jax
import jax.numpy as jnp
from jax import lax
from jax.experimental import pallas as pl
from jax.experimental.pallas import tpu as pltpu
from jax.sharding import PartitionSpec as P

FB_X = 2
FB_Y = 2
MESH = pl.DeviceIdType.MESH
BF = jnp.bfloat16
F32 = jnp.float32
DIRS = ((-1, 0), (1, 0), (0, -1), (0, 1), (-1, -1), (-1, 1), (1, -1), (1, 1))
OPPOSITE = tuple(DIRS.index((-dx, -dy)) for dx, dy in DIRS)
NT = (((1,), (1,)), ((), ()))


def dot(a, b, dims=(((1,), (0,)), ((), ()))):
    return lax.dot_general(a, b, dims, preferred_element_type=F32)


def iota(shape, dim):
    return lax.broadcasted_iota(jnp.int32, shape, dim)


def one_hot(cond):
    return jnp.where(cond, 1.0, 0.0).astype(BF)


def identity(n):
    return one_hot(iota((n, n), 0) == iota((n, n), 1))


def child_row(v):
    p, q, s = v >> 6, (v >> 3) & 7, v & 7
    k = 4 * (p & 1) + 2 * (q & 1) + (s & 1)
    return k * 64 + (p >> 1) * 16 + (q >> 1) * 4 + (s >> 1)


def octant_column(u, meta, m):
    return (
        64 * (4 * meta[m, 3] + (u >> 4))
        + 8 * (4 * meta[m, 4] + ((u >> 2) & 3))
        + 4 * meta[m, 5]
        + (u & 3)
    )


def padded_rows(block, width):
    extra = width - block.shape[0]
    if extra == 0:
        return block
    return jnp.concatenate([block, jnp.zeros((extra, block.shape[1]), block.dtype)], 0)


class Exchange:
    def __init__(self, sizes, face_send, face_recv, edge_send, edge_recv, send_sem, recv_sem):
        gx, gy = lax.axis_index("gx"), lax.axis_index("gy")
        nx, ny = sizes
        self.refs = (face_send, face_recv, edge_send, edge_recv)
        self.sems = (send_sem, recv_sem)
        self.there, self.target = [], []
        for dx, dy in DIRS:
            x, y = gx + dx, gy + dy
            self.there.append((x >= 0) & (x < nx) & (y >= 0) & (y < ny))
            self.target.append((x, y))

    def greet(self, others):
        barrier = pltpu.get_barrier_semaphore()
        for d in range(8):
            @pl.when(self.there[d])
            def _():
                pl.semaphore_signal(barrier, inc=1, device_id=self.target[d], device_id_type=MESH)

        for target in others:
            pl.semaphore_signal(barrier, inc=1, device_id=target, device_id_type=MESH)

    def await_greetings(self, others):
        peers = len(others) + sum(there.astype(jnp.int32) for there in self.there)
        pl.semaphore_wait(pltpu.get_barrier_semaphore(), peers)

    def copy(self, d, landing):
        face_send, face_recv, edge_send, edge_recv = self.refs
        send, recv = (face_send, face_recv) if d < 4 else (edge_send, edge_recv)
        return pltpu.make_async_remote_copy(
            src_ref=send.at[d % 4],
            dst_ref=recv.at[landing % 4],
            send_sem=self.sems[0].at[d],
            recv_sem=self.sems[1].at[landing],
            device_id=self.target[d],
            device_id_type=MESH,
        )

    def pack(self, own, info):
        face_send, face_recv, edge_send, edge_recv = self.refs
        for d, (dx, dy) in enumerate(DIRS):
            x = 7 if dx > 0 else 0
            y = 7 if dy > 0 else 0
            if d < 2:
                face_send[d, 0:8] = own[8 * x : 8 * x + 8]
            elif d < 4:
                for i in range(8):
                    face_send[d, i] = own[8 * i + y]
            else:
                edge_send[d - 4, 0] = own[8 * x + y]
            if d < 4:
                face_send[d, 8:11] = info
            else:
                edge_send[d - 4, 1:4] = info

    def start(self):
        _, face_recv, _, edge_recv = self.refs
        for d in range(8):
            @pl.when(self.there[d])
            def _():
                self.copy(d, OPPOSITE[d]).start()

            @pl.when(jnp.logical_not(self.there[d]))
            def _():
                recv = face_recv if d < 4 else edge_recv
                recv[d % 4] = jnp.zeros(recv.shape[1:], recv.dtype)

    def finish(self):
        for d in range(8):
            @pl.when(self.there[d])
            def _():
                copy = self.copy(d, d)
                copy.wait_send()
                copy.wait_recv()


def weights_of(place, meta, m, dx, dy):
    x, y, z = place
    base = [meta[m, i].astype(F32) for i in range(3)]
    same = (x == base[0] + float(dx)) & (y == base[1] + float(dy))
    step = z - base[2]
    here = jnp.where(same & (step == 0.0), 1.0, 0.0)
    below = jnp.where(same & (step == -1.0), 1.0, 0.0)
    above = jnp.where(same & (step == 1.0), 1.0, 0.0)
    level = iota(here.shape, 0)
    return jnp.where(level == 7, below, here), here, jnp.where(level == 0, above, here)


def rolled(block, step):
    flat = block.reshape(-1, 8, block.shape[-1])
    return pltpu.roll(flat, step, 1).reshape(block.shape)


def sum_sources(sources):
    total = None
    for block, weights in sources:
        terms = [block if weight is None else block * weight for weight in weights]
        total = terms if total is None else [a + b for a, b in zip(total, terms)]
    return rolled(total[0], 1), total[1], rolled(total[2], 7)


def put(window, at_x, at_y, per_slot):
    width = per_slot[0][0].shape[-1]
    for k in range(3):
        both = jnp.concatenate([parts[k] for parts in per_slot], 1).astype(BF)
        rows = both.shape[0]
        if at_x is None:
            for i in range(rows):
                window[i + 1, at_y, :, k * width : (k + 1) * width] = both[i]
        elif at_y is None:
            window[at_x, 1 : 1 + rows, :, k * width : (k + 1) * width] = both
        else:
            window[at_x, at_y, :, k * width : (k + 1) * width] = both[0]


def own_place(meta, s, width):
    return [jnp.full((8, width), meta[s, i].astype(F32), F32) for i in range(3)]


def build_centre(window, own, meta, slots):
    width = own.shape[-1]
    ones = jnp.ones((8, width), F32)
    level = iota((8, width), 0)
    self_weights = (jnp.where(level == 7, 0.0, ones), None, jnp.where(level == 0, 0.0, ones))
    other = [
        [(s, weights_of(own_place(meta, s, width), meta, m, 0, 0)) for s in range(slots) if s != m]
        for m in range(slots)
    ]

    def step(x, carry):
        rows = own[pl.ds(8 * x, 8)].astype(F32)
        blocks = [rows[:, 8 * s : 8 * s + 8] for s in range(slots)]
        per_slot = []
        for m in range(slots):
            sources = [(blocks[m], self_weights)] + [(blocks[s], w) for s, w in other[m]]
            per_slot.append(sum_sources(sources))
        put(window, x + 1, None, per_slot)
        return carry

    lax.fori_loop(0, 8, step, 0)


def build_border(window, own, face_recv, edge_recv, meta, slots):
    width = own.shape[-1]
    for dx, dy in DIRS:
        x = {-1: 7, 0: None, 1: 0}[dx]
        y = {-1: 7, 0: None, 1: 0}[dy]
        if dx and dy:
            own_rows = own[8 * x + y][None]
        elif dx:
            own_rows = own[8 * x : 8 * x + 8]
        else:
            own_rows = jnp.stack([own[8 * i + y] for i in range(8)], 0)
        own_rows = own_rows.astype(F32)
        tiles = []
        if dx:
            ref, d = face_recv, DIRS.index((dx, 0))
            rows = ref[d, y : y + 1] if dy else ref[d, 0:8]
            tiles.append((rows, ref[d, 8:11], dx, 0))
        if dy:
            ref, d = face_recv, DIRS.index((0, dy))
            rows = ref[d, x : x + 1] if dx else ref[d, 0:8]
            tiles.append((rows, ref[d, 8:11], 0, dy))
        if dx and dy:
            d = DIRS.index((dx, dy)) - 4
            tiles.append((edge_recv[d, 0:1], edge_recv[d, 1:4], dx, dy))
        tiles = [(rows.astype(F32), info.astype(F32), tx, ty) for rows, info, tx, ty in tiles]
        per_slot = []
        for m in range(slots):
            sources = []
            for s in range(slots):
                span = slice(8 * s, 8 * s + 8)
                if s != m:
                    place = own_place(meta, s, width)
                    sources.append((own_rows[:, span], weights_of(place, meta, m, dx, dy)))
                for rows, info, tx, ty in tiles:
                    place = (
                        info[0, span] + float(FB_X * tx),
                        info[1, span] + float(FB_Y * ty),
                        info[2, span],
                    )
                    sources.append((rows[:, span], weights_of(place, meta, m, dx, dy)))
            per_slot.append(sum_sources(sources))
        put(
            window,
            None if not dx else (0 if dx < 0 else 9),
            None if not dy else (0 if dy < 0 else 9),
            per_slot,
        )


def patch(window, j):
    x, y = j // 3, j % 3
    view = window[pl.ds(x, 8), pl.ds(y, 8)]
    return view.reshape(64 * view.shape[2], view.shape[3])


class Ring:
    def __init__(self, index, count, target, send_sem, recv_sem):
        self.index, self.count = index, count
        self.sems = (send_sem, recv_sem)
        self.ranks = [lax.rem(index + r, count) for r in range(1, count)]
        self.origins = [lax.rem(index + count - r, count) for r in range(1, count)]
        self.targets = [target(rank) for rank in self.ranks]

    def copies(self, source, landing):
        return [
            pltpu.make_async_remote_copy(
                src_ref=source(i, self.ranks[i]),
                dst_ref=landing(i, self.index),
                send_sem=self.sems[0].at[i],
                recv_sem=self.sems[1].at[i],
                device_id=self.targets[i],
                device_id_type=MESH,
            )
            for i in range(self.count - 1)
        ]

    def start(self, source, landing):
        for copy in self.copies(source, landing):
            copy.start()

    def finish(self, source, arrived):
        sends = self.copies(source, arrived)
        for i, copy in enumerate(sends):
            copy.wait_send()
            pltpu.make_async_remote_copy(
                src_ref=source(i, self.ranks[i]),
                dst_ref=arrived(i, self.origins[i]),
                send_sem=self.sems[0].at[i],
                recv_sem=self.sems[1].at[i],
                device_id=self.targets[i],
                device_id_type=MESH,
            ).wait_recv()


def add_rows(target, own, arrived, count, low, high, step):
    def body(i, carry):
        at = pl.multiple_of(low + i * step, 16)
        total = own(at).astype(F32)
        for r in range(count):
            total = total + arrived[r, pl.ds(at, step)].astype(F32)
        target(at, total.astype(BF))
        return carry

    lax.fori_loop(0, (high - low) // step, body, 0)


def store_to(ref, base):
    def store(at, value):
        ref[pl.ds(pl.multiple_of(base + at, 16), value.shape[0])] = value

    return store


def load_from(ref, base, step):
    return lambda at: ref[pl.ds(pl.multiple_of(base + at, 16), step)]


class Part:
    def __init__(self, order, chunk, base, sems, summed, partial, final, arrivals):
        (i, count, to_one), (j, others, to_two) = order
        self.i, self.j, self.chunk, self.base = i, j, chunk, base
        self.summed, self.partial, self.final = summed, partial, final
        self.arrivals = arrivals
        self.part = part = chunk * others
        self.mine = base + (i * others + j) * chunk
        self.rings = [
            Ring(i, count, to_one, *sems[0]),
            Ring(j, others, to_two, *sems[1]),
            Ring(j, others, to_two, *sems[2]),
            Ring(i, count, to_one, *sems[3]),
        ]
        wide = lambda r: pl.ds(pl.multiple_of(base + r * part, 16), part)
        thin = lambda r: pl.ds(pl.multiple_of(r * chunk, 16), chunk)
        cell = lambda r: pl.ds(pl.multiple_of(base + (i * others + r) * chunk, 16), chunk)
        self.source = [
            lambda n, r: summed.at[wide(r)],
            lambda n, r: partial.at[thin(r)],
            lambda n, r: final.at[cell(j)],
            lambda n, r: final.at[wide(i)],
        ]
        self.land = [
            lambda n, r: arrivals[0].at[n],
            lambda n, r: arrivals[1].at[n],
            lambda n, r: final.at[cell(r)],
            lambda n, r: final.at[wide(r)],
        ]

    def begin(self, n):
        self.rings[n].start(self.source[n], self.land[n])

    def end(self, n):
        self.rings[n].finish(self.source[n], self.land[n])

    def start_first(self):
        self.begin(0)

    def start_second(self):
        self.end(0)
        add_rows(
            store_to(self.partial, 0), load_from(self.summed, self.base + self.i * self.part, self.chunk),
            self.arrivals[0], self.rings[0].count - 1, 0, self.part, self.chunk,
        )
        self.begin(1)

    def start_third(self):
        self.end(1)
        add_rows(
            store_to(self.final, self.mine), load_from(self.partial, self.j * self.chunk, 16),
            self.arrivals[1], self.rings[1].count - 1, 0, self.chunk, 16,
        )
        self.begin(2)

    def start_fourth(self):
        self.end(2)
        self.begin(3)

    def finish(self):
        self.end(3)


class Plan:
    def __init__(self, sizes, channels):
        self.nx, self.ny = sizes
        self.inner = 4 if self.nx % 4 == 0 else 1
        self.outer = self.nx // self.inner
        self.rows = channels // self.ny
        self.padded = -(-self.rows // 16) * 16
        self.full = channels // 128
        self.tail = channels % 128
        self.per = 128 // self.tail if self.tail else 1
        self.groups = -(-27 // self.per) if self.tail else 0
        total = (27 * self.full + self.groups) * self.padded
        self.chunk = -(-total // (16 * self.nx)) * 16
        self.total = self.chunk * self.nx
        self.used = total
        self.blocks, at, starts = [], 0, {}
        for first in range(0, 27, self.per):
            es = list(range(first, min(27, first + self.per)))
            starts[first] = at
            for e in es:
                for tile in range(self.full):
                    self.blocks.append(([e], tile, at))
                    at += self.padded
            if self.tail:
                self.blocks.append((es, None, at))
                at += self.padded
        self.steps = (0, 4, 6, 9)
        ends = [0]
        for bound in self.steps[1:-1]:
            ends.append(max(row for e, row in starts.items() if e <= 3 * bound))
        ends.append(self.total)
        self.spans = list(zip(ends[:-1], ends[1:]))
        across = self.chunk // 48 * 16 if min(self.inner, self.outer) > 1 else 0
        self.chunks = [self.chunk - across] + ([across] if across else [])


def pack_weight_gradient(plan, stage, wide, width, span):
    rows, padded = plan.rows, plan.padded

    def piece(e, share, low, high):
        j, k = e // 3, e % 3
        value = wide[j, share * rows : (share + 1) * rows, k * width + low : k * width + high]
        if padded != rows:
            value = jnp.concatenate([value, jnp.zeros((padded - rows, high - low), F32)], 0)
        return value

    low, high = span
    for share in range(plan.ny):
        for es, tile, at in plan.blocks:
            if not low <= at < high:
                continue
            if tile is not None:
                block = piece(es[0], share, 128 * tile, 128 * tile + 128)
            else:
                base = 128 * plan.full
                parts = [piece(e, share, base, base + plan.tail) for e in es]
                left = 128 - plan.tail * len(es)
                if left:
                    parts.append(jnp.zeros((padded, left), F32))
                block = jnp.concatenate(parts, 1)
            stage[share, at : at + padded] = block.astype(BF)
        if high == plan.total and plan.used < plan.total:
            stage[share, plan.used :] = jnp.zeros((plan.total - plan.used, 128), BF)


def unpack_weight_gradient(plan, final, out):
    rows, padded, tail = plan.rows, plan.padded, plan.tail
    for es, tile, at in plan.blocks:
        block = final[at : at + padded].astype(F32)[:rows]
        if tile is not None:
            out[es[0], :, 128 * tile : 128 * tile + 128] = block
        else:
            for i, e in enumerate(es):
                out[e, :, 128 * plan.full :] = block[:, i * tail : (i + 1) * tail]


def whole_kernel(
    sizes, plan, fine, coarse_place, parents, counts, skip, coarse, cot, up_raw, weight_raw,
    grad_skip, grad_coarse, grad_rows,
    own, window, acc, turned, up, weight, fetched, held, wide, stage, summed, partial, final,
    in_y, arrivals, fetch_sem,
    face_send, face_recv, edge_send, edge_recv, send_sem, recv_sem,
    face_send2, face_recv2, edge_send2, edge_recv2, send_sem2, recv_sem2,
    ring_send, ring_recv,
):
    slots, channels, voxels = skip.shape
    width = own.shape[-1]
    gx, gy = lax.axis_index("gx"), lax.axis_index("gy")
    first = Exchange(sizes, face_send, face_recv, edge_send, edge_recv, send_sem, recv_sem)
    second = Exchange(sizes, face_send2, face_recv2, edge_send2, edge_recv2, send_sem2, recv_sem2)
    inner, outer = plan.inner, plan.outer
    a, b = lax.rem(gx, inner), lax.div(gx, inner)

    def sems(i):
        return ring_send.at[i], ring_recv.at[i]

    rings_y = [Ring(gy, plan.ny, lambda r: (gx, r), *sems(i)) for i in (0, 9, 10)]
    to_inner = lambda r: (b * inner + r, gy)
    to_outer = lambda r: (r * inner + a, gy)
    groups = ((a, inner, to_inner), (b, outer, to_outer))
    base, parts = 0, []
    for number, chunk in enumerate(plan.chunks):
        order = groups if number == 0 else groups[::-1]
        parts.append(
            Part(order, chunk, base, [sems(1 + 4 * number + i) for i in range(4)],
                 summed, partial[number], final, arrivals[2 * number : 2 * number + 2])
        )
        base += chunk * plan.nx
    others = rings_y[0].targets + parts[0].rings[0].targets + parts[0].rings[1].targets
    first.greet(others)
    fetches = [
        pltpu.make_async_copy(weight_raw, fetched, fetch_sem.at[0]),
        pltpu.make_async_copy(cot, held, fetch_sem.at[1]),
    ]
    for fetch in fetches:
        fetch.start()

    meta = {}
    for m in range(slots):
        parent = parents[m]
        for i in range(3):
            base = sum(
                jnp.where(parent == n, coarse_place[n, i], 0) for n in range(coarse.shape[0])
            )
            meta[m, i] = fine[m, i]
            meta[m, 3 + i] = fine[m, i] - 2 * base
        meta[m, 6] = parent
        meta[m, 7] = jnp.where(m < counts[0], 1, 0)
    info = jnp.stack(
        [
            jnp.concatenate(
                [jnp.full((8, width), meta[m, i].astype(F32), F32) for m in range(slots)], 0
            )
            for i in range(3)
        ],
        0,
    ).astype(BF)

    up[...] = jnp.zeros_like(up)
    for k in range(8):
        up[k * width : k * width + channels, 0:channels] = up_raw[k]
    eye = identity(voxels)
    spread = one_hot(iota((voxels, voxels), 1) == child_row(iota((voxels, 1), 0)))
    rows = []
    for m in range(slots):
        octant = None
        column = octant_column(iota((64, 1), 0), meta, m)
        for n in range(coarse.shape[0]):
            pick = one_hot(iota((64, voxels), 1) == jnp.where(meta[m, 6] == n, column, -1))
            part = dot(pick, padded_rows(coarse[n], width), NT)
            octant = part if octant is None else octant + part
        lifted = dot(octant.astype(BF), up[...], NT)
        lifted = jnp.concatenate([lifted[:, k * width : (k + 1) * width] for k in range(8)], 0)
        high = lifted.astype(BF)
        low = (lifted - high.astype(F32)).astype(BF)
        total = dot(spread, high) + dot(spread, low) + dot(eye, padded_rows(skip[m], width), NT)
        rows.append((total * meta[m, 7].astype(F32)).reshape(64, 8, width))
    own[...] = jnp.concatenate(rows, 1).astype(BF)
    first.pack(own, info)
    first.await_greetings(others)
    first.start()
    weight[...] = jnp.zeros_like(weight)
    fetches[0].wait()
    for e in range(27):
        low = (e % 3) * width
        weight[e // 3, 0:channels, low : low + channels] = fetched[e]
    build_centre(window, own, meta, slots)
    first.finish()
    build_border(window, own, face_recv, edge_recv, meta, slots)
    acc[...] = jnp.zeros_like(acc)

    def conv(j, carry):
        acc[...] += dot(patch(window, j), weight[j], NT)
        return carry

    lax.fori_loop(0, 9, conv, 0)
    pre_all = acc[...].reshape(64, 8 * slots, width)
    grads = []
    fetches[1].wait()
    for m in range(slots):
        pre = pre_all[:, 8 * m : 8 * m + 8].reshape(voxels, width)
        sigma = 1.0 / (1.0 + jnp.exp(-pre))
        value = dot(eye, padded_rows(held[m], width), NT)
        value = value * (sigma * (1.0 + pre * (1.0 - sigma))) * meta[m, 7].astype(F32)
        grads.append(value.reshape(64, 8, width))
    grad = jnp.concatenate(grads, 1)
    own[...] = grad.astype(BF)
    second.pack(own, info)
    second.start()
    turned[...] = jnp.transpose(grad.reshape(64 * 8 * slots, width)).astype(BF)

    def outer_product(j, carry):
        wide[j] = dot(turned[...], patch(window, j))
        return carry

    sends = []
    for number, (low, high) in enumerate(plan.spans):
        lax.fori_loop(plan.steps[number], plan.steps[number + 1], outer_product, 0)
        pack_weight_gradient(plan, stage, wide, width, (low, high))
        rows_of = pl.ds(low, high - low)
        source_y = lambda i, r, rows_of=rows_of: stage.at[r, rows_of]
        land_y = lambda i, r, rows_of=rows_of: in_y.at[i, rows_of]
        rings_y[number].start(source_y, land_y)
        sends.append((rings_y[number], source_y, land_y))
    build_centre(window, own, meta, slots)
    for ring, source_y, land_y in sends:
        ring.finish(source_y, land_y)
    for part in parts:
        add_rows(
            store_to(summed, 0), lambda at: stage[gy, pl.ds(at, part.chunk)],
            in_y, plan.ny - 1, part.base, part.base + part.chunk * plan.nx, part.chunk,
        )
        part.start_first()

    second.finish()
    build_border(window, own, face_recv2, edge_recv2, meta, slots)
    acc[...] = jnp.zeros_like(acc)

    def conv_back(j, carry):
        rows = patch(window, j)
        value = None
        for k in range(3):
            term = dot(
                rows[:, k * width : (k + 1) * width],
                weight[8 - j, :, (2 - k) * width : (3 - k) * width],
            )
            value = term if value is None else value + term
        acc[...] += value
        return carry

    lax.fori_loop(0, 4, conv_back, 0)
    for part in parts:
        part.start_second()
    lax.fori_loop(4, 9, conv_back, 0)
    for part in parts:
        part.start_third()

    all_rows = acc[...].reshape(64, 8 * slots, width)
    gather = one_hot(iota((voxels, voxels), 0) == child_row(iota((1, voxels), 1)))
    folded = []
    for m in range(slots):
        rows = all_rows[:, 8 * m : 8 * m + 8].reshape(voxels, width) * meta[m, 7].astype(F32)
        grad_skip[m] = jnp.transpose(rows).astype(BF)[:channels]
        grouped = dot(gather, rows.astype(BF)).astype(BF)
        folded.append(jnp.concatenate([grouped[64 * k : 64 * k + 64] for k in range(8)], 1))

    for part in parts:
        part.start_fourth()
    folded = [jnp.transpose(dot(grouped, up[...])).astype(BF) for grouped in folded]
    for n in range(grad_coarse.shape[0]):
        value = None
        for m in range(slots):
            column = octant_column(iota((64, 1), 0), meta, m)
            place = one_hot(iota((64, voxels), 1) == jnp.where(meta[m, 6] == n, column, -1))
            term = dot(folded[m], place)
            value = term if value is None else value + term
        grad_coarse[n] = value.astype(BF)[:channels]
    for part in parts:
        part.finish()
    grad_rows[...] = final[...]


def output_kernel(plan, skip_in, coarse_in, rows_in, skip_out, coarse_out, conv_out):
    skip_out[...] = skip_in[...]
    coarse_out[...] = coarse_in[...]
    unpack_weight_gradient(plan, rows_in, conv_out)


def exchange_scratch(slots, width):
    return [
        pltpu.VMEM((4, 11, 8 * slots, width), BF),
        pltpu.VMEM((4, 11, 8 * slots, width), BF),
        pltpu.VMEM((4, 4, 8 * slots, width), BF),
        pltpu.VMEM((4, 4, 8 * slots, width), BF),
        pltpu.SemaphoreType.DMA((8,)),
        pltpu.SemaphoreType.DMA((8,)),
    ]


def local(
    sizes, skip_feature_rows, coarse_features, cotangent, fine_coords, coarse_coords,
    parents, counts, conv_weight, up_weight,
):
    slots, channels, voxels = skip_feature_rows.shape
    width = -(-channels // 128) * 128
    plan = Plan(sizes, channels)
    peers = max(plan.ny, plan.inner, plan.outer, 2) - 1
    smem = pl.BlockSpec(memory_space=pltpu.SMEM)
    vmem = pl.BlockSpec(memory_space=pltpu.VMEM)
    anywhere = pl.BlockSpec(memory_space=pl.ANY)
    cells = 64 * 8 * slots
    partials, arrivals = [], []
    for number, chunk in enumerate(plan.chunks):
        sides = (plan.inner, plan.outer) if number == 0 else (plan.outer, plan.inner)
        partials.append(pltpu.VMEM((chunk * sides[1], 128), BF))
        arrivals.append(pltpu.VMEM((max(sides[0] - 1, 1), chunk * sides[1], 128), BF))
        arrivals.append(pltpu.VMEM((max(sides[1] - 1, 1), chunk, 128), BF))
    grad_skip, grad_coarse, grad_rows = pl.pallas_call(
        functools.partial(whole_kernel, sizes, plan),
        out_shape=(
            jax.ShapeDtypeStruct((slots, channels, voxels), BF),
            jax.ShapeDtypeStruct(coarse_features.shape, BF),
            jax.ShapeDtypeStruct((plan.total, 128), BF),
        ),
        in_specs=[smem] * 4 + [vmem, vmem, anywhere, vmem, anywhere],
        out_specs=(vmem, vmem, vmem),
        scratch_shapes=[
            pltpu.VMEM((64, 8 * slots, width), BF),
            pltpu.VMEM((10, 10, 8 * slots, 3 * width), BF),
            pltpu.VMEM((cells, width), F32),
            pltpu.VMEM((width, cells), BF),
            pltpu.VMEM((8 * width, width), BF),
            pltpu.VMEM((9, width, 3 * width), BF),
            pltpu.VMEM((27, channels, channels), BF),
            pltpu.VMEM((slots, channels, voxels), BF),
            pltpu.VMEM((9, width, 3 * width), F32),
            pltpu.VMEM((plan.ny, plan.total, 128), BF),
            pltpu.VMEM((plan.total, 128), BF),
            tuple(partials),
            pltpu.VMEM((plan.total, 128), BF),
            pltpu.VMEM((max(plan.ny - 1, 1), plan.total, 128), BF),
            tuple(arrivals),
            pltpu.SemaphoreType.DMA((2,)),
        ]
        + exchange_scratch(slots, width)
        + exchange_scratch(slots, width)
        + [pltpu.SemaphoreType.DMA((11, peers)), pltpu.SemaphoreType.DMA((11, peers))],
        compiler_params=pltpu.CompilerParams(
            collective_id=0, has_side_effects=True, vmem_limit_bytes=60 * 1024 * 1024
        ),
        cost_estimate=pl.CostEstimate(
            flops=6 * 27 * slots * voxels * channels * channels,
            bytes_accessed=12 << 20, transcendentals=0,
        ),
        name="whole",
    )(
        fine_coords, coarse_coords, parents, counts,
        skip_feature_rows, coarse_features, cotangent, up_weight,
        conv_weight.transpose(1, 0, 2),
    )
    grad_skip, grad_coarse, grad_conv = pl.pallas_call(
        functools.partial(output_kernel, plan),
        out_shape=(
            jax.ShapeDtypeStruct(grad_skip.shape, BF),
            jax.ShapeDtypeStruct(grad_coarse.shape, BF),
            jax.ShapeDtypeStruct((27, plan.rows, channels), F32),
        ),
        in_specs=[vmem] * 3,
        out_specs=(vmem, vmem, vmem),
        compiler_params=pltpu.CompilerParams(vmem_limit_bytes=60 * 1024 * 1024),
        name="outputs",
    )(grad_skip, grad_coarse, grad_rows)
    return (grad_skip, grad_coarse, grad_conv.transpose(1, 0, 2))


def solution(mesh):
    in_specs = (
        P(("gx", "gy"), None, None),
        P(("gx", "gy"), None, None),
        P(("gx", "gy"), None, None),
        P(("gx", "gy"), None),
        P(("gx", "gy"), None),
        P(("gx", "gy")),
        P(("gx", "gy")),
        P(),
        P(),
    )
    out_specs = (P(("gx", "gy"), None, None), P(("gx", "gy"), None, None), P("gy", None, None))
    sizes = (mesh.shape["gx"], mesh.shape["gy"])
    return jax.shard_map(
        functools.partial(local, sizes),
        mesh=mesh,
        in_specs=in_specs,
        out_specs=out_specs,
        check_vma=False,
    )
```
